32 devices in a mesh: groups: 2 (over y), panel: 4 (over x, core), tok: 4 (over z).
Axes of the slice: x: 2, y: 2, z: 4, core: 2. Of those that a mesh axis runs over, the one named last changes fastest.
Arguments:
- grads: bfloat16 [768, 5120], P(('groups', 'tok'), 'panel'), parts along dimension 0, may hold values from -6 to 6
- acts: bfloat16 [768, 5120], P(('groups', 'panel'), 'tok'), parts along dimension 0, may hold values from -6 to 6
- out_basis: bfloat16 [5120, 5120], P('panel', 'tok'), may hold values from -0.078125 to 0.078125
- in_basis: bfloat16 [5120, 5120], P('tok', 'panel'), may hold values from -0.078125 to 0.078125
- query_rot: bfloat16 [5120, 8, 5120], P('tok', None, 'panel'), may hold values from -0.0011672974 to 0.0011672974
- eigvals: float32 [5120, 5120], P('tok', 'panel'), may hold values from 0.1 to 10
Outputs:
- influence: float32 [768, 8], P(('groups', 'panel', 'tok')), parts along dimension 0
The draws below stay inside these ranges and needn't reach their ends.
There are 2 independent parts, one for each index of `groups`. The reference program is written for one: setup_inputs(seed, part) draws one part's arguments, and reference() takes and returns one part's arrays. A program takes and returns all parts, laid end to end along the dimension named above; an argument that names none is the same for every part. Nothing has to cross between parts.
All inputs are finite; a program needn't handle non-finite values.
Results may differ from the reference program's by a relative error of at most 0.0051.
Values may be sent and summed in bfloat16 or wider, within the bound.
No kernel may reach another device: no remote copies, remote signals or barrier semaphores. Data moves between devices by JAX's collectives and lax.ppermute only.
A program may use at most 256 MiB of HBM per device.

```python
import math
import jax
import jax.numpy as jnp
from jax import lax

D = 5120
QUERIES = 8
TOKENS = 384


def shard_levels(stream_key, shape, cuts, smallest, high):
    loudness = 1.0
    for position, parts in cuts:
        draws = jax.random.uniform(jax.random.fold_in(jax.random.fold_in(stream_key, 6), position), (parts,), jnp.float32, smallest / len(cuts), high / len(cuts))
        loudness = loudness * jnp.repeat(jnp.exp(draws), shape[position] // parts).reshape((-1,) + (1,) * (len(shape) - 1 - position))
    return loudness


def gaussian(key, extent, deviation, limit, pieces=(), kind=jnp.bfloat16):
    entries = deviation * jax.random.normal(key, extent, jnp.float32)
    if pieces:
        entries = entries * shard_levels(key, extent, pieces, -0.22, 0.18)
    return jnp.clip(entries, -limit, limit).astype(kind)


def setup_inputs(seed: int = 0, part: int = 0) -> dict:
    splits = jax.random.split(jax.random.key(seed), 7)
    part_keys = jax.random.split(jax.random.fold_in(splits[6], part), 7)
    grads = gaussian(part_keys[0], (TOKENS, D), 1.0, 6.0, ((0, 4), (1, 4)))
    acts = gaussian(part_keys[1], (TOKENS, D), 1.0, 6.0, ((0, 4), (1, 4)))
    out_basis = gaussian(splits[2], (D, D), D ** -0.5, 0.078125, ((0, 4), (1, 4)))
    in_basis = gaussian(splits[3], (D, D), D ** -0.5, 0.078125, ((0, 4), (1, 4)))
    query_rot = gaussian(splits[4], (D, QUERIES, D), (1.0 / D), 0.0011672974, ((0, 4), (2, 4)))
    eigvals = jnp.clip(jnp.exp(math.log(10.0) - 4.6051702 * jax.random.uniform(splits[5], (D, D), jnp.float32) ** shard_levels(splits[5], (D, D), ((0, 4), (1, 4)), -0.2, 0.2)), 0.1, 10.0)
    return dict(grads=grads, acts=acts, out_basis=out_basis, in_basis=in_basis, query_rot=query_rot, eigvals=eigvals)


DAMPING = 0.1


def reference(grads, acts, out_basis, in_basis, query_rot, eigvals):
    grad_rot = jnp.dot(grads.astype(jnp.float32), out_basis.astype(jnp.float32), precision=lax.Precision.HIGHEST).astype(jnp.bfloat16)
    act_rot = jnp.dot(acts.astype(jnp.float32), in_basis.astype(jnp.float32), precision=lax.Precision.HIGHEST).astype(jnp.bfloat16)
    grad_rot = lax.optimization_barrier(grad_rot)
    act_rot = lax.optimization_barrier(act_rot)
    grad_wide = grad_rot.astype(jnp.float32)
    act_wide = act_rot.astype(jnp.float32)
    shifted = eigvals + DAMPING

    def one_query(query_slice):
        precond = (query_slice.astype(jnp.float32) / shifted).astype(jnp.bfloat16)
        precond = lax.optimization_barrier(precond)
        mixed_terms = jnp.dot(grad_wide, precond.astype(jnp.float32), precision=lax.Precision.HIGHEST)
        return jnp.sum(mixed_terms * act_wide, axis=1)

    scores = lax.map(one_query, jnp.moveaxis(query_rot, 1, 0))
    return jnp.transpose(scores)
```

```python
import math

import jax
import jax.numpy as jnp
from jax import lax
from jax.experimental import pallas as pl
from jax.experimental.pallas import tpu as pltpu
from jax.sharding import PartitionSpec as P

DAMPING = 0.1
WIDE = jnp.float32
NARROW = jnp.bfloat16


def swap(value, axis, mask):
    size = lax.axis_size(axis)
    return lax.ppermute(value, axis, [(i, i ^ mask) for i in range(size)])


def gather_panel(acts):
    if lax.axis_size("panel") != 4:
        return lax.all_gather(acts, "panel", axis=0, tiled=True)
    near = swap(acts, "panel", 1)
    far = swap(acts, "panel", 2)
    both = swap(far, "panel", 1)
    place = lax.axis_index("panel")
    blocks = (acts, near, far, both)
    return jnp.concatenate([lax.select_n(place ^ b, *blocks) for b in range(4)], axis=0)


def gather_tok(grads):
    if lax.axis_size("tok") != 4:
        return lax.all_gather(grads, "tok", axis=0, tiled=True)
    up = lax.ppermute(grads, "tok", [(i, (i + 1) % 4) for i in range(4)])
    down = lax.ppermute(grads, "tok", [(i, (i + 3) % 4) for i in range(4)])
    half = grads.shape[0] // 2
    up_far = lax.ppermute(up[:half], "tok", [(i, (i + 1) % 4) for i in range(4)])
    down_far = lax.ppermute(down[half:], "tok", [(i, (i + 3) % 4) for i in range(4)])
    far = jnp.concatenate([up_far, down_far], axis=0)
    place = lax.axis_index("tok")
    blocks = (grads, down, far, up)
    return jnp.concatenate([lax.select_n((b - place + 4) % 4, *blocks) for b in range(4)], axis=0)


def sum_tok(part):
    if lax.axis_size("tok") != 4:
        return lax.psum(part, "tok").astype(NARROW)
    half = part.shape[0] // 2
    outs = []
    for rows, order in ((part[:half], (1, 3)), (part[half:], (3, 1))):
        for mask in order:
            rows = rows + swap(rows.astype(NARROW), "tok", mask).astype(WIDE)
        outs.append(rows.astype(NARROW))
    return jnp.concatenate(outs, axis=0)


def sum_panel(part):
    if lax.axis_size("panel") != 4:
        return lax.psum(part, "panel").astype(NARROW)
    half = part.shape[0] // 2
    core = lax.axis_index("panel") % 2
    top, bottom = part[:half], part[half:]
    first = core == 0
    mine = jnp.where(first, top, bottom)
    other = jnp.where(first, bottom, top).astype(NARROW)
    mine = mine + swap(other, "panel", 1).astype(WIDE)
    mine = mine + swap(mine.astype(NARROW), "panel", 2).astype(WIDE)
    mine = mine.astype(NARROW)
    other = swap(mine, "panel", 1)
    return jnp.concatenate([jnp.where(first, mine, other), jnp.where(first, other, mine)], axis=0)


def precond_kernel(query_ref, eig_ref, out_ref):
    rows, queries, cols = query_ref.shape
    scale = 1.0 / (eig_ref[...] + DAMPING)
    value = query_ref[...].astype(WIDE) * scale[:, None, :]
    out_ref[...] = value.reshape(rows * queries, cols).astype(NARROW)


def precondition(query_rot, eigvals):
    depth, queries, cols = query_rot.shape
    step = math.gcd(depth, 64)
    return pl.pallas_call(
        precond_kernel,
        grid=(depth // step,),
        in_specs=[
            pl.BlockSpec((step, queries, cols), lambda i: (i, 0, 0)),
            pl.BlockSpec((step, cols), lambda i: (i, 0)),
        ],
        out_specs=pl.BlockSpec((step * queries, cols), lambda i: (i, 0)),
        out_shape=jax.ShapeDtypeStruct((depth * queries, cols), NARROW),
        compiler_params=pltpu.CompilerParams(vmem_limit_bytes=40 * 1024 * 1024),
        cost_estimate=pl.CostEstimate(
            flops=2 * depth * queries * cols,
            bytes_accessed=4 * depth * queries * cols + 4 * depth * cols,
            transcendentals=0,
        ),
        name="precondition",
    )(query_rot, eigvals)


def score_kernel(pre_ref, act_ref, grad_ref, out_ref, act_turned, grad_turned):
    step = pl.program_id(0)
    queries, tokens = out_ref.shape
    block = pre_ref.shape[0] // queries

    @pl.when(step == 0)
    def _():
        act_turned[...] = act_ref[...].astype(WIDE).T.astype(NARROW)
        grad_turned[...] = grad_ref[...].astype(WIDE).T
        out_ref[...] = jnp.zeros_like(out_ref)

    mixed = jnp.dot(pre_ref[...], act_turned[...], preferred_element_type=WIDE)
    grad = grad_turned[pl.ds(pl.multiple_of(step * block, block), block), :]
    mixed = mixed.reshape(block, queries, tokens) * grad[:, None, :]
    out_ref[...] += jnp.sum(mixed, axis=0)


def scores(precond, act_rot, grad_rot, queries):
    total, cols = precond.shape
    tokens, depth = grad_rot.shape
    step = math.gcd(depth, 64)
    return pl.pallas_call(
        score_kernel,
        grid=(depth // step,),
        in_specs=[
            pl.BlockSpec((step * queries, cols), lambda i: (i, 0)),
            pl.BlockSpec((tokens, cols), lambda i: (0, 0)),
            pl.BlockSpec((tokens, depth), lambda i: (0, 0)),
        ],
        out_specs=pl.BlockSpec((queries, tokens), lambda i: (0, 0)),
        out_shape=jax.ShapeDtypeStruct((queries, tokens), WIDE),
        scratch_shapes=[pltpu.VMEM((cols, tokens), NARROW), pltpu.VMEM((depth, tokens), WIDE)],
        compiler_params=pltpu.CompilerParams(vmem_limit_bytes=40 * 1024 * 1024),
        cost_estimate=pl.CostEstimate(
            flops=2 * total * cols * tokens, bytes_accessed=2 * total * cols, transcendentals=0
        ),
        name="scores",
    )(precond, act_rot, grad_rot)


def per_device(grads, acts, out_basis, in_basis, query_rot, eigvals):
    acts_all = gather_panel(acts)
    grads_all = gather_tok(grads)
    precond = precondition(query_rot, eigvals)
    act_part = jnp.dot(acts_all, in_basis, preferred_element_type=WIDE)
    grad_part = jnp.dot(grads_all, out_basis, preferred_element_type=WIDE)
    act_rot = sum_tok(act_part)
    grad_rot = sum_panel(grad_part)
    queries = query_rot.shape[1]
    partial = scores(precond, act_rot, grad_rot, queries)
    owners = lax.axis_size("panel") * lax.axis_size("tok")
    tokens = partial.shape[1]
    split = partial.reshape(queries, owners, tokens // owners).transpose(1, 0, 2)
    got = lax.all_to_all(split, ("panel", "tok"), split_axis=0, concat_axis=0, tiled=True)
    return jnp.sum(got, axis=0).T


def solution(mesh):
    placed = (
        P(("groups", "tok"), "panel"),
        P(("groups", "panel"), "tok"),
        P("panel", "tok"),
        P("tok", "panel"),
        P("tok", None, "panel"),
        P("tok", "panel"),
    )
    return jax.shard_map(
        per_device,
        mesh=mesh,
        in_specs=placed,
        out_specs=P(("groups", "panel", "tok"), None),
        check_vma=False,
    )
```

```python
import functools
import math

import jax
import jax.numpy as jnp
from jax import lax
from jax.experimental import pallas as pl
from jax.experimental.pallas import tpu as pltpu
from jax.sharding import PartitionSpec as P

DAMPING = 0.1
WIDE = jnp.float32
NARROW = jnp.bfloat16
ROOM = 48 * 1024 * 1024


def swap(value, axis, mask):
    return lax.ppermute(value, axis, [(i, i ^ mask) for i in range(lax.axis_size(axis))])


def dot(a, b):
    return jnp.dot(a, b, preferred_element_type=WIDE)


def chain_sum(part):
    into = lax.ppermute(part.astype(NARROW), "tok", [(0, 1), (3, 2)])
    half = part + into.astype(WIDE)
    across = lax.ppermute(half.astype(NARROW), "tok", [(1, 2), (2, 1)])
    total = (half + across.astype(WIDE)).astype(NARROW)
    back = lax.ppermute(total, "tok", [(1, 0), (2, 3)])
    return total, back


def rotate_kernel(place_ref, b0, b1, b2, b3, basis_ref, mine_ref, other_ref, rows_ref):
    size = b0.shape[0]
    half = mine_ref.shape[0]
    for k, block in enumerate((b0, b1, b2, b3)):
        rows_ref[pl.ds(pl.multiple_of(place_ref[k] * size, size), size), :] = block[...]
    core = place_ref[4]
    mine = rows_ref[pl.ds(pl.multiple_of(core * half, half), half), :]
    other = rows_ref[pl.ds(pl.multiple_of((1 - core) * half, half), half), :]
    other_ref[...] = dot(other, basis_ref[...]).astype(NARROW)
    mine_ref[...] = dot(mine, basis_ref[...])


def rotate(places, blocks, basis):
    size, depth = blocks[0].shape
    width = basis.shape[1]
    whole = pl.BlockSpec(memory_space=pltpu.VMEM)
    return pl.pallas_call(
        rotate_kernel,
        in_specs=[pl.BlockSpec(memory_space=pltpu.SMEM)] + [whole] * 5,
        out_specs=[whole, whole],
        out_shape=[
            jax.ShapeDtypeStruct((2 * size, width), WIDE),
            jax.ShapeDtypeStruct((2 * size, width), NARROW),
        ],
        scratch_shapes=[pltpu.VMEM((4 * size, depth), NARROW)],
        compiler_params=pltpu.CompilerParams(vmem_limit_bytes=ROOM),
        cost_estimate=pl.CostEstimate(
            flops=8 * size * depth * width, bytes_accessed=2 * depth * width, transcendentals=0
        ),
        name="rotate",
    )(places, *blocks, basis)


def sum_panel(mine, other):
    mine = mine + swap(other, "panel", 1).astype(WIDE)
    mine = (mine + swap(mine.astype(NARROW), "panel", 2).astype(WIDE)).astype(NARROW)
    return mine, swap(mine, "panel", 1)


def score_kernel(chunks, spot_ref, query_ref, eig_ref, *refs):
    act_refs, (grad_mine, grad_other), (out_ref, act_rows, act_turned, grad_rows, grad_turned) = (
        refs[: 2 * chunks],
        refs[2 * chunks : 2 * chunks + 2],
        refs[2 * chunks + 2 :],
    )
    step = pl.program_id(0)
    block, queries, cols = query_ref.shape
    tokens = out_ref.shape[1]
    piece = math.gcd(block, 32)

    @pl.when(step == 0)
    def _():
        for k in range(chunks):
            size = act_refs[k].shape[0]
            rows = pl.ds(pl.multiple_of(spot_ref[k] * size, size), size)

            @pl.when(spot_ref[chunks] == 1)
            def _():
                act_rows[rows, :] = act_refs[k][...].astype(WIDE)

            @pl.when(spot_ref[chunks] == 0)
            def _():
                act_rows[rows, :] = act_refs[chunks + k][...].astype(WIDE)

        act_turned[...] = act_rows[...].T.astype(NARROW)
        half = grad_mine.shape[0]
        core = spot_ref[chunks + 1]
        grad_rows[pl.ds(pl.multiple_of(core * half, half), half), :] = grad_mine[...].astype(WIDE)
        grad_rows[pl.ds(pl.multiple_of((1 - core) * half, half), half), :] = grad_other[...].astype(WIDE)
        grad_turned[...] = grad_rows[...].T
        out_ref[...] = jnp.zeros_like(out_ref)

    total = out_ref[...]
    for k in range(block // piece):
        scale = 1.0 / (eig_ref[k * piece : (k + 1) * piece, :] + DAMPING)
        query = query_ref[k * piece : (k + 1) * piece].astype(WIDE) * scale[:, None, :]
        precond = query.reshape(piece * queries, cols).astype(NARROW)
        mixed = dot(precond, act_turned[...]).reshape(piece, queries, tokens)
        grad = grad_turned[pl.ds(pl.multiple_of(step * block + k * piece, piece), piece), :]
        total = total + jnp.sum(mixed * grad[:, None, :], axis=0)
    out_ref[...] = total


def scores(spots, acts, grads, query_rot, eigvals):
    depth, queries, cols = query_rot.shape
    chunks = len(acts) // 2
    tokens = chunks * acts[0].shape[0]
    step = math.gcd(depth, 256)
    whole = pl.BlockSpec(memory_space=pltpu.VMEM)
    return pl.pallas_call(
        functools.partial(score_kernel, chunks),
        grid=(depth // step,),
        in_specs=[
            pl.BlockSpec(memory_space=pltpu.SMEM),
            pl.BlockSpec((step, queries, cols), lambda i: (i, 0, 0)),
            pl.BlockSpec((step, cols), lambda i: (i, 0)),
        ]
        + [whole] * (len(acts) + 2),
        out_specs=pl.BlockSpec((queries, tokens), lambda i: (0, 0)),
        out_shape=jax.ShapeDtypeStruct((queries, tokens), WIDE),
        scratch_shapes=[
            pltpu.VMEM((tokens, cols), WIDE),
            pltpu.VMEM((cols, tokens), NARROW),
            pltpu.VMEM((tokens, depth), WIDE),
            pltpu.VMEM((depth, tokens), WIDE),
        ],
        compiler_params=pltpu.CompilerParams(vmem_limit_bytes=ROOM),
        cost_estimate=pl.CostEstimate(
            flops=2 * depth * queries * cols * tokens,
            bytes_accessed=2 * depth * queries * cols + 4 * depth * cols,
            transcendentals=0,
        ),
        name="scores",
    )(spots, query_rot, eigvals, *acts, *grads)


def on_lines_of_four(grads, acts, out_basis, in_basis):
    panel, tok = lax.axis_index("panel"), lax.axis_index("tok")
    near = swap(acts, "panel", 1)
    far = swap(acts, "panel", 2)
    grad_blocks = [grads] + [swap(grads, "tok", mask) for mask in (1, 3, 2)]
    act_chunks = [acts, near, far, swap(far, "panel", 1)]
    sums = [chain_sum(dot(chunk, in_basis)) for chunk in act_chunks]
    act_rot = [total for total, _ in sums] + [back for _, back in sums]
    places = jnp.stack([tok, tok ^ 1, tok ^ 3, tok ^ 2, panel % 2]).astype(jnp.int32)
    grad_rot = sum_panel(*rotate(places, grad_blocks, out_basis))
    middle = ((tok == 1) | (tok == 2)).astype(jnp.int32)
    spots = jnp.stack([panel, panel ^ 1, panel ^ 2, panel ^ 3, middle, panel % 2]).astype(jnp.int32)
    return spots, act_rot, grad_rot


def on_any(grads, acts, out_basis, in_basis):
    acts_all = lax.all_gather(acts, "panel", axis=0, tiled=True)
    grads_all = lax.all_gather(grads, "tok", axis=0, tiled=True)
    act_rot = lax.psum(dot(acts_all, in_basis), "tok").astype(NARROW)
    grad_rot = lax.psum(dot(grads_all, out_basis), "panel").astype(NARROW)
    half = grad_rot.shape[0] // 2
    spots = jnp.array([0, 1, 0], jnp.int32)
    return spots, [act_rot, act_rot], (grad_rot[:half], grad_rot[half:])


def per_device(grads, acts, out_basis, in_basis, query_rot, eigvals):
    small = lax.axis_size("panel") == 4 and lax.axis_size("tok") == 4
    rotated = on_lines_of_four if small else on_any
    spots, act_rot, grad_rot = rotated(grads, acts, out_basis, in_basis)
    partial = scores(spots, act_rot, grad_rot, query_rot, eigvals)
    queries, tokens = partial.shape
    owners = lax.axis_size("panel") * lax.axis_size("tok")
    split = partial.reshape(queries, owners, tokens // owners).transpose(1, 0, 2)
    got = lax.all_to_all(split, ("panel", "tok"), split_axis=0, concat_axis=0, tiled=True)
    return jnp.sum(got, axis=0).T


def solution(mesh):
    placed = (
        P(("groups", "tok"), "panel"),
        P(("groups", "panel"), "tok"),
        P("panel", "tok"),
        P("tok", "panel"),
        P("tok", None, "panel"),
        P("tok", "panel"),
    )
    return jax.shard_map(
        per_device,
        mesh=mesh,
        in_specs=placed,
        out_specs=P(("groups", "panel", "tok"), None),
        check_vma=False,
    )
```

```python
import functools
import math

import jax
import jax.numpy as jnp
from jax import lax
from jax.experimental import pallas as pl
from jax.experimental.pallas import tpu as pltpu
from jax.sharding import PartitionSpec as P

DAMPING = 0.1
WIDE = jnp.float32
NARROW = jnp.bfloat16
ROOM = 48 * 1024 * 1024
LANES = 128
SLOTS = 3
KEPT = 1 << 20
IN_VMEM = pl.BlockSpec(memory_space=pltpu.VMEM)
IN_SMEM = pl.BlockSpec(memory_space=pltpu.SMEM)
ANYWHERE = pl.BlockSpec(memory_space=pl.ANY)


def swap(value, axis, mask):
    return lax.ppermute(value, axis, [(i, i ^ mask) for i in range(lax.axis_size(axis))])


def dot(a, b):
    return jnp.dot(a, b, preferred_element_type=WIDE)


class Steps:
    def __init__(self):
        self.last = None

    def __call__(self, name, body, ins, outs, scalars=None, scratch=(), room=16 * 1024 * 1024, flops=0, streamed=(), after=()):
        def block(x):
            if math.prod(x.shape) > KEPT:
                return IN_VMEM
            return pl.BlockSpec(x.shape, lambda i: (0,) * len(x.shape))

        def home(x):
            if math.prod(x.shape) > KEPT:
                return pltpu.with_memory_space_constraint(x, pltpu.VMEM)
            return pltpu.with_memory_space_constraint(x, pltpu.HBM) if x.dtype == WIDE else x

        def result(x):
            if math.prod(x.shape) > KEPT:
                return pltpu.VMEM(x.shape, x.dtype)
            return x

        streamed = [pltpu.with_memory_space_constraint(x, pltpu.HBM) for x in streamed]
        specs, args = [], []
        if scalars is not None:
            specs.append(IN_SMEM)
            args.append(scalars)
        specs += [block(x) for x in ins] + [ANYWHERE] * len(streamed)
        args += [home(x) for x in ins] + streamed
        kept = len(args)
        ties = list(after) + ([] if self.last is None else [self.last])
        specs += [ANYWHERE] * len(ties)
        args += ties
        given = len(args)

        def kernel(*refs):
            body(*refs[:kept], *refs[given:])

        moved = sum(math.prod(x.shape) * x.dtype.itemsize for x in [*ins, *outs, *streamed])
        results = pl.pallas_call(
            kernel,
            grid=(1,),
            in_specs=specs,
            out_specs=[block(x) for x in outs],
            out_shape=[result(x) for x in outs],
            scratch_shapes=list(scratch),
            compiler_params=pltpu.CompilerParams(vmem_limit_bytes=room),
            cost_estimate=pl.CostEstimate(flops=flops, bytes_accessed=moved, transcendentals=0),
            name=name,
        )(*args)
        self.last = results[-1]
        return results


def load_body(*refs):
    count = len(refs) // 2
    sems = refs[-1]
    copies = [pltpu.make_async_copy(refs[k], refs[count + k], sems.at[k]) for k in range(count)]
    for copy in copies:
        copy.start()
    for copy in copies:
        copy.wait()


def send_body(turn_ref, a_ref, b_ref, basis_ref, send_ref, rows_ref):
    pick(turn_ref[0], b_ref, a_ref, rows_ref)
    send_ref[...] = dot(rows_ref[...], basis_ref[...]).astype(NARROW)


def pick(turn, zero_ref, one_ref, rows_ref):
    @pl.when(turn == 0)
    def _():
        rows_ref[...] = zero_ref[...]

    @pl.when(turn == 1)
    def _():
        rows_ref[...] = one_ref[...]


def pair_body(turn_ref, a_ref, b_ref, basis_ref, got_ref, out_ref, rows_ref):
    pick(turn_ref[0], a_ref, b_ref, rows_ref)
    out_ref[...] = (dot(rows_ref[...], basis_ref[...]) + got_ref[...].astype(WIDE)).astype(NARROW)


def pass_body(a_ref, out_ref):
    out_ref[...] = a_ref[...]


def mark_body(out_ref):
    out_ref[...] = jnp.zeros_like(out_ref)


def add_body(a_ref, b_ref, out_ref):
    out_ref[...] = (a_ref[...].astype(WIDE) + b_ref[...].astype(WIDE)).astype(NARROW)


def rotate_body(place_ref, b0, b1, b2, b3, basis_ref, mine_ref, top_ref, low_ref, rows_ref):
    size = b0.shape[0]
    half = 2 * size
    for k, block in enumerate((b0, b1, b2, b3)):
        rows_ref[pl.ds(pl.multiple_of(place_ref[k] * size, size), size), :] = block[...]
    core = place_ref[4]
    other = dot(rows_ref[pl.ds(pl.multiple_of((1 - core) * half, half), half), :], basis_ref[...])
    top_ref[...] = other[:size].astype(NARROW)
    low_ref[...] = other[size:].astype(NARROW)
    mine_ref[...] = dot(rows_ref[pl.ds(pl.multiple_of(core * half, half), half), :], basis_ref[...])


def chip_sum_body(core_ref, mine_ref, top_pair, low_pair, wide_ref, top_out, low_out):
    size = top_out.shape[0]
    source = pl.ds(pl.multiple_of((1 - core_ref[0]) * size, size), size)
    for k, (pair, out) in enumerate(((top_pair, top_out), (low_pair, low_out))):
        rows = slice(k * size, (k + 1) * size)
        value = mine_ref[rows, :] + pair[source, :].astype(WIDE)
        wide_ref[rows, :] = value
        out[...] = value.astype(NARROW)


def panel_sum_body(wide_ref, top_ref, low_ref, top_out, low_out):
    half = top_ref.shape[0]
    top_out[...] = (wide_ref[:half, :] + top_ref[...].astype(WIDE)).astype(NARROW)
    low_out[...] = (wide_ref[half:, :] + low_ref[...].astype(WIDE)).astype(NARROW)


def score_body(
    spot_ref, a0, a1, a2, a3, mine_top, mine_low, other_top, other_low, query_ref, eig_ref, out_ref,
    act_ref, grad_ref, query_buf, eig_buf, sems
):
    depth, queries, cols = query_ref.shape
    tokens = out_ref.shape[1]
    count = depth // LANES

    def copies(k):
        slot = lax.rem(k, SLOTS)
        rows = pl.ds(pl.multiple_of(k * LANES, LANES), LANES)
        return (
            pltpu.make_async_copy(query_ref.at[rows], query_buf.at[slot], sems.at[slot, 0]),
            pltpu.make_async_copy(eig_ref.at[rows], eig_buf.at[slot], sems.at[slot, 1]),
        )

    for k in range(SLOTS - 1):
        for copy in copies(k):
            copy.start()

    size = tokens // 4
    for k, block in enumerate((a0, a1, a2, a3)):
        act_ref[pl.ds(pl.multiple_of(spot_ref[k] * size, size), size), :] = block[...]
    core = spot_ref[4]
    for first, refs in ((core, (mine_top, mine_low)), (1 - core, (other_top, other_low))):
        for k, ref in enumerate(refs):
            grad_ref[pl.ds(pl.multiple_of((2 * first + k) * size, size), size), :] = ref[...]

    group = LANES // queries
    lane = lax.broadcasted_iota(jnp.int32, (tokens, LANES), 1) // queries

    def step(k, total):
        @pl.when(k + SLOTS - 1 < count)
        def _():
            for copy in copies(k + SLOTS - 1):
                copy.start()

        for copy in copies(k):
            copy.wait()
        slot = lax.rem(k, SLOTS)
        start = pl.multiple_of(k * LANES, LANES)
        scale = 1.0 / (eig_buf[slot] + DAMPING)
        query = query_buf[slot].astype(WIDE) * scale[:, None, :]
        precond = query.reshape(LANES * queries, cols).astype(NARROW)
        mixed = lax.dot_general(
            act_ref[...], precond, (((1,), (1,)), ((), ())), preferred_element_type=WIDE
        )
        grad = grad_ref[:, pl.ds(start, LANES)].astype(WIDE)
        for part in range(queries):
            spread = jnp.take_along_axis(grad, lane + part * group, axis=1)
            total = total + mixed[:, part * LANES : (part + 1) * LANES] * spread
        return total

    total = lax.fori_loop(0, count, step, jnp.zeros((tokens, LANES), WIDE))
    shift = LANES // 2
    while shift >= queries:
        total = total + pltpu.roll(total, shift, 1)
        shift //= 2
    out_ref[...] = total.T[:queries, :]


def spread_out(partial):
    queries, tokens = partial.shape
    owners = lax.axis_size("panel") * lax.axis_size("tok")
    split = partial.reshape(queries, owners, tokens // owners).transpose(1, 0, 2)
    return lax.all_to_all(split, ("panel", "tok"), split_axis=0, concat_axis=0, tiled=True)


def on_lines_of_four(grads, acts, out_basis, in_basis, query_rot, eigvals):
    size, feats = grads.shape
    depth, queries, cols = query_rot.shape
    panel, tok = lax.axis_index("panel"), lax.axis_index("tok")
    core, turn = panel % 2, tok % 2
    steps = Steps()

    def wide(rows, width):
        return jax.ShapeDtypeStruct((rows, width), WIDE)

    def narrow(rows, width):
        return jax.ShapeDtypeStruct((rows, width), NARROW)

    def scalars(*values):
        return jnp.stack(values).astype(jnp.int32)

    g1, g3 = swap(grads, "tok", 1), swap(grads, "tok", 3)
    near = swap(acts, "panel", 1)
    far = swap(acts, "panel", 2)
    most = swap(acts, "panel", 3)

    def loaded(name, *arrays):
        return steps(
            name, load_body, [], [narrow(*x.shape) for x in arrays],
            scratch=[pltpu.SemaphoreType.DMA((len(arrays),))], streamed=arrays,
        )

    (in_basis,) = loaded("load_in", in_basis)
    one = [pltpu.VMEM((size, feats), NARROW)]
    cost = 2 * size * feats * cols
    (send1,) = steps(
        "send_near", send_body, [acts, near, in_basis], [narrow(size, cols)], scalars=scalars(turn), scratch=one, flops=cost
    )
    got1 = swap(send1, "tok", 1)
    (send2,) = steps(
        "send_far", send_body, [far, most, in_basis], [narrow(size, cols)], scalars=scalars(turn), scratch=one, flops=cost
    )
    got2 = swap(send2, "tok", 1)
    (g3,) = steps("pass", pass_body, [g3], [narrow(size, feats)], after=[g1])
    g2 = swap(g3, "tok", 1)
    (pair1,) = steps(
        "pair_near", pair_body, [acts, near, in_basis, got1], [narrow(size, cols)], scalars=scalars(turn), scratch=one, flops=cost
    )
    got1 = swap(pair1, "tok", 2)
    (pair2,) = steps(
        "pair_far", pair_body, [far, most, in_basis, got2], [narrow(size, cols)], scalars=scalars(turn), scratch=one, flops=cost
    )
    got2 = swap(pair2, "tok", 2)
    (out_basis,) = loaded("load_out", out_basis)
    mine, top, low = steps(
        "rotate", rotate_body, [grads, g1, g3, g2, out_basis],
        [wide(2 * size, depth), narrow(size, depth), narrow(size, depth)],
        scalars=scalars(tok, tok ^ 1, tok ^ 3, tok ^ 2, core),
        scratch=[pltpu.VMEM((4 * size, feats), NARROW)], flops=8 * size * feats * depth,
    )
    chips = [[2 * k, 2 * k + 1] for k in range(2)]
    top, low = (lax.all_gather(x, "panel", axis=0, tiled=True, axis_index_groups=chips) for x in (top, low))
    mine, top, low = steps(
        "chip_sum", chip_sum_body, [mine, top, low],
        [wide(2 * size, depth), narrow(size, depth), narrow(size, depth)], scalars=scalars(core),
    )
    top, low = swap(top, "panel", 2), swap(low, "panel", 2)
    (total1,) = steps("total_near", add_body, [pair1, got1], [narrow(size, cols)])
    back1 = swap(total1, "tok", 1)
    (total2,) = steps("total_far", add_body, [pair2, got2], [narrow(size, cols)])
    back2 = swap(total2, "tok", 1)
    mine_top, mine_low = steps("panel_sum", panel_sum_body, [mine, top, low], [narrow(size, depth)] * 2)
    other_top, other_low = swap(mine_top, "panel", 1), swap(mine_low, "panel", 1)
    steps("mark", mark_body, [], [wide(8, LANES)], after=[back1, back2])
    (partial,) = steps(
        "scores", score_body, [total1, back1, total2, back2, mine_top, mine_low, other_top, other_low],
        [wide(queries, 4 * size)],
        scalars=scalars(panel ^ turn, panel ^ turn ^ 1, panel ^ turn ^ 2, panel ^ turn ^ 3, core),
        scratch=[
            pltpu.VMEM((4 * size, cols), NARROW),
            pltpu.VMEM((4 * size, depth), NARROW),
            pltpu.VMEM((SLOTS, LANES, queries, cols), NARROW),
            pltpu.VMEM((SLOTS, LANES, cols), WIDE),
            pltpu.SemaphoreType.DMA((SLOTS, 2)),
        ],
        room=28 * 1024 * 1024, flops=8 * size * depth * queries * cols, streamed=[query_rot, eigvals],
    )
    return jnp.sum(spread_out(partial), axis=0).T


def any_score_kernel(query_ref, eig_ref, act_ref, grad_ref, out_ref, act_turned, grad_turned):
    step = pl.program_id(0)
    block, queries, cols = query_ref.shape
    tokens = out_ref.shape[1]
    piece = math.gcd(block, 32)

    @pl.when(step == 0)
    def _():
        act_turned[...] = act_ref[...].astype(WIDE).T.astype(NARROW)
        grad_turned[...] = grad_ref[...].astype(WIDE).T
        out_ref[...] = jnp.zeros_like(out_ref)

    total = out_ref[...]
    for k in range(block // piece):
        scale = 1.0 / (eig_ref[k * piece : (k + 1) * piece, :] + DAMPING)
        query = query_ref[k * piece : (k + 1) * piece].astype(WIDE) * scale[:, None, :]
        precond = query.reshape(piece * queries, cols).astype(NARROW)
        mixed = dot(precond, act_turned[...]).reshape(piece, queries, tokens)
        grad = grad_turned[pl.ds(pl.multiple_of(step * block + k * piece, piece), piece), :]
        total = total + jnp.sum(mixed * grad[:, None, :], axis=0)
    out_ref[...] = total


def on_any(grads, acts, out_basis, in_basis, query_rot, eigvals):
    acts_all = lax.all_gather(acts, "panel", axis=0, tiled=True)
    grads_all = lax.all_gather(grads, "tok", axis=0, tiled=True)
    act_rot = lax.psum(dot(acts_all, in_basis), "tok").astype(NARROW)
    grad_rot = lax.psum(dot(grads_all, out_basis), "panel").astype(NARROW)
    depth, queries, cols = query_rot.shape
    tokens = act_rot.shape[0]
    step = math.gcd(depth, 256)
    partial = pl.pallas_call(
        any_score_kernel,
        grid=(depth // step,),
        in_specs=[
            pl.BlockSpec((step, queries, cols), lambda i: (i, 0, 0)),
            pl.BlockSpec((step, cols), lambda i: (i, 0)),
            IN_VMEM,
            IN_VMEM,
        ],
        out_specs=pl.BlockSpec((queries, tokens), lambda i: (0, 0)),
        out_shape=jax.ShapeDtypeStruct((queries, tokens), WIDE),
        scratch_shapes=[pltpu.VMEM((cols, tokens), NARROW), pltpu.VMEM((depth, tokens), WIDE)],
        compiler_params=pltpu.CompilerParams(vmem_limit_bytes=ROOM),
        name="any_scores",
    )(query_rot, eigvals, act_rot, grad_rot)
    return jnp.sum(spread_out(partial), axis=0).T


def per_device(*arrays):
    four = lax.axis_size("panel") == 4 and lax.axis_size("tok") == 4
    return (on_lines_of_four if four else on_any)(*arrays)


def solution(mesh):
    placed = (
        P(("groups", "tok"), "panel"),
        P(("groups", "panel"), "tok"),
        P("panel", "tok"),
        P("tok", "panel"),
        P("tok", None, "panel"),
        P("tok", "panel"),
    )
    return jax.shard_map(
        per_device,
        mesh=mesh,
        in_specs=placed,
        out_specs=P(("groups", "panel", "tok"), None),
        check_vma=False,
    )
```

```python
import functools
import math

import jax
import jax.numpy as jnp
from jax import lax
from jax.experimental import pallas as pl
from jax.experimental.pallas import tpu as pltpu
from jax.sharding import PartitionSpec as P

DAMPING = 0.1
WIDE = jnp.float32
NARROW = jnp.bfloat16
ROOM = 48 * 1024 * 1024
LANES = 128
SLOTS = 3
KEPT = 1 << 19
IN_VMEM = pl.BlockSpec(memory_space=pltpu.VMEM)
IN_SMEM = pl.BlockSpec(memory_space=pltpu.SMEM)
ANYWHERE = pl.BlockSpec(memory_space=pl.ANY)


def swap(value, axis, mask):
    return lax.ppermute(value, axis, [(i, i ^ mask) for i in range(lax.axis_size(axis))])


def dot(a, b):
    return jnp.dot(a, b, preferred_element_type=WIDE)


class Steps:
    def __init__(self):
        self.last = None

    def __call__(self, name, body, ins, outs, scalars=None, scratch=(), room=16 * 1024 * 1024, flops=0, streamed=(), where=(), after=(), weight=0):
        def block(x):
            if math.prod(x.shape) > KEPT:
                return IN_VMEM
            return pl.BlockSpec(x.shape, lambda i: (0,) * len(x.shape))

        def home(x):
            if math.prod(x.shape) > KEPT:
                return pltpu.with_memory_space_constraint(x, pltpu.VMEM)
            return x

        def result(x):
            if math.prod(x.shape) > KEPT:
                return pltpu.VMEM(x.shape, x.dtype)
            return x

        streamed = [pltpu.with_memory_space_constraint(x, pltpu.HBM) for x in streamed]
        specs, args = [], []
        if scalars is not None:
            specs.append(IN_SMEM)
            args.append(scalars)
        specs += [block(x) for x in ins] + [ANYWHERE] * (len(streamed) + len(where))
        args += [home(x) for x in ins] + streamed + list(where)
        kept = len(args)
        ties = list(after) + ([] if self.last is None else [self.last])
        specs += [ANYWHERE] * len(ties)
        args += ties
        given = len(args)

        def kernel(*refs):
            body(*refs[:kept], *refs[given:])

        moved = weight + sum(math.prod(x.shape) * x.dtype.itemsize for x in [*ins, *outs, *streamed])
        results = pl.pallas_call(
            kernel,
            grid=(1,),
            in_specs=specs,
            out_specs=[block(x) for x in outs],
            out_shape=[result(x) for x in outs],
            scratch_shapes=list(scratch),
            compiler_params=pltpu.CompilerParams(vmem_limit_bytes=room),
            cost_estimate=pl.CostEstimate(flops=flops, bytes_accessed=moved, transcendentals=0),
            name=name,
        )(*args)
        self.last = results[-1]
        return results


def load_body(*refs):
    count = len(refs) // 2
    sems = refs[-1]
    copies = [pltpu.make_async_copy(refs[k], refs[count + k], sems.at[k]) for k in range(count)]
    for copy in copies:
        copy.start()
    for copy in copies:
        copy.wait()


def load_send_body(turn_ref, basis_ref, a_ref, b_ref, held, send_ref, rows_ref, sem, sems):
    blocks = fetch(basis_ref, held, sems)
    pick(turn_ref[0], b_ref, a_ref, rows_ref, sem)
    total = None
    for rows, copy in blocks:
        copy.wait()
        value = dot(rows_ref[:, rows], held[rows, :])
        total = value if total is None else total + value
    send_ref[...] = total.astype(NARROW)


def fetch(source, held, sems):
    count = sems.shape[0]
    size = source.shape[0] // count
    found = []
    for k in range(count):
        rows = pl.ds(k * size, size)
        copy = pltpu.make_async_copy(source.at[rows], held.at[rows], sems.at[k])
        copy.start()
        found.append((rows, copy))
    return found


def send_body(turn_ref, basis_ref, a_ref, b_ref, send_ref, rows_ref, sem):
    pick(turn_ref[0], b_ref, a_ref, rows_ref, sem)
    send_ref[...] = dot(rows_ref[...], basis_ref[...]).astype(NARROW)


def pick(turn, zero_ref, one_ref, rows_ref, sem):
    @pl.when(turn == 0)
    def _():
        copy = pltpu.make_async_copy(zero_ref, rows_ref, sem)
        copy.start()
        copy.wait()

    @pl.when(turn == 1)
    def _():
        copy = pltpu.make_async_copy(one_ref, rows_ref, sem)
        copy.start()
        copy.wait()


def pair_body(turn_ref, basis_ref, got_ref, a_ref, b_ref, out_ref, rows_ref, sem):
    pick(turn_ref[0], a_ref, b_ref, rows_ref, sem)
    out_ref[...] = (dot(rows_ref[...], basis_ref[...]) + got_ref[...].astype(WIDE)).astype(NARROW)


def pass_body(a_ref, out_ref):
    out_ref[...] = a_ref[...]


def mark_body(out_ref):
    out_ref[...] = jnp.zeros_like(out_ref)


def add_body(a_ref, b_ref, out_ref):
    out_ref[...] = (a_ref[...].astype(WIDE) + b_ref[...].astype(WIDE)).astype(NARROW)


def rotate_body(place_ref, b0, b1, b2, b3, basis_ref, mine_top, mine_low, top_ref, low_ref, rows_ref):
    size = b0.shape[0]
    half = 2 * size
    for k, block in enumerate((b0, b1, b2, b3)):
        rows_ref[pl.ds(pl.multiple_of(place_ref[k] * size, size), size), :] = block[...]
    core = place_ref[4]
    other = dot(rows_ref[pl.ds(pl.multiple_of((1 - core) * half, half), half), :], basis_ref[...])
    top_ref[...] = other[:size].astype(NARROW)
    low_ref[...] = other[size:].astype(NARROW)
    mine = dot(rows_ref[pl.ds(pl.multiple_of(core * half, half), half), :], basis_ref[...])
    mine_top[...] = mine[:size]
    mine_low[...] = mine[size:]


def chip_sum_body(core_ref, mine_ref, pair_ref, *refs):
    given = (len(refs) - 2) // 2
    wide_ref, out_ref = refs[given], refs[given + 1]
    size = out_ref.shape[0]
    source = pl.ds(pl.multiple_of((1 - core_ref[0]) * size, size), size)
    value = mine_ref[...] + pair_ref[source, :].astype(WIDE)
    wide_ref[...] = value
    out_ref[...] = value.astype(NARROW)
    for k in range(given):
        refs[given + 2 + k][...] = refs[k][...]


def panel_sum_body(wide_ref, got_ref, out_ref):
    out_ref[...] = (wide_ref[...] + got_ref[...].astype(WIDE)).astype(NARROW)


def score_body(
    spot_ref, a0, a1, a2, a3, mine_top, mine_low, other_top, other_low, query_ref, eig_ref, out_ref,
    act_ref, grad_ref, query_buf, eig_buf, sems
):
    depth, queries, cols = query_ref.shape
    owners = out_ref.shape[0]
    tokens = 4 * a0.shape[0]
    count = depth // LANES

    def copies(k):
        slot = lax.rem(k, SLOTS)
        rows = pl.ds(pl.multiple_of(k * LANES, LANES), LANES)
        return (
            pltpu.make_async_copy(query_ref.at[rows], query_buf.at[slot], sems.at[slot, 0]),
            pltpu.make_async_copy(eig_ref.at[rows], eig_buf.at[slot], sems.at[slot, 1]),
        )

    for k in range(SLOTS - 1):
        for copy in copies(k):
            copy.start()

    size = tokens // 4
    for k, block in enumerate((a0, a1, a2, a3)):
        act_ref[pl.ds(pl.multiple_of(spot_ref[k] * size, size), size), :] = block[...]
    core = spot_ref[4]
    for first, refs in ((core, (mine_top, mine_low)), (1 - core, (other_top, other_low))):
        for k, ref in enumerate(refs):
            grad_ref[pl.ds(pl.multiple_of((2 * first + k) * size, size), size), :] = ref[...]

    group = LANES // queries
    lane = lax.broadcasted_iota(jnp.int32, (tokens, LANES), 1) // queries

    def step(k, total):
        @pl.when(k + SLOTS - 1 < count)
        def _():
            for copy in copies(k + SLOTS - 1):
                copy.start()

        for copy in copies(k):
            copy.wait()
        slot = lax.rem(k, SLOTS)
        start = pl.multiple_of(k * LANES, LANES)
        scale = 1.0 / (eig_buf[slot] + DAMPING)
        query = query_buf[slot].astype(WIDE) * scale[:, None, :]
        precond = query.reshape(LANES * queries, cols).astype(NARROW)
        mixed = lax.dot_general(
            act_ref[...], precond, (((1,), (1,)), ((), ())), preferred_element_type=WIDE
        )
        grad = grad_ref[:, pl.ds(start, LANES)].astype(WIDE)
        for part in range(queries):
            spread = jnp.take_along_axis(grad, lane + part * group, axis=1)
            total = total + mixed[:, part * LANES : (part + 1) * LANES] * spread
        return total

    total = lax.fori_loop(0, count, step, jnp.zeros((tokens, LANES), WIDE))
    shift = LANES // 2
    while shift >= queries:
        total = total + pltpu.roll(total, shift, 1)
        shift //= 2
    turned = total.T[:queries, :]
    owned = tokens // owners
    for k in range(owners):
        out_ref[k, :, :owned] = turned[:, k * owned : (k + 1) * owned]


def final_body(got_ref, out_ref):
    out_ref[...] = jnp.sum(got_ref[...], axis=0)[:, : out_ref.shape[1]]


def spread_out(partial):
    queries, tokens = partial.shape
    owners = lax.axis_size("panel") * lax.axis_size("tok")
    split = partial.reshape(queries, owners, tokens // owners).transpose(1, 0, 2)
    return lax.all_to_all(split, ("panel", "tok"), split_axis=0, concat_axis=0, tiled=True)


def on_lines_of_four(grads, acts, out_basis, in_basis, query_rot, eigvals):
    size, feats = grads.shape
    depth, queries, cols = query_rot.shape
    panel, tok = lax.axis_index("panel"), lax.axis_index("tok")
    core, turn = panel % 2, tok % 2
    steps = Steps()

    def wide(*shape):
        return jax.ShapeDtypeStruct(shape, WIDE)

    def narrow(*shape):
        return jax.ShapeDtypeStruct(shape, NARROW)

    def scalars(*values):
        return jnp.stack(values).astype(jnp.int32)

    g1, g3 = swap(grads, "tok", 1), swap(grads, "tok", 2)
    near = swap(acts, "panel", 1)
    far = swap(acts, "panel", 2)
    most = swap(acts, "panel", 3)

    def loaded(name, *arrays):
        return steps(
            name, load_body, [], [narrow(*x.shape) for x in arrays],
            scratch=[pltpu.SemaphoreType.DMA((len(arrays),))], streamed=arrays,
        )

    one = [pltpu.VMEM((size, feats), NARROW), pltpu.SemaphoreType.DMA]
    cost = 2 * size * feats * cols
    options = dict(scalars=scalars(turn), scratch=one, flops=cost)
    acts = pltpu.with_memory_space_constraint(acts, pltpu.HBM)
    in_basis, send1 = steps(
        "send_near", load_send_body, [], [narrow(*in_basis.shape), narrow(size, cols)], scalars=scalars(turn),
        scratch=one + [pltpu.SemaphoreType.DMA((4,))], flops=cost, streamed=[in_basis], where=[acts, pltpu.with_memory_space_constraint(near, pltpu.HBM)],
    )
    got1 = swap(send1, "tok", 1)
    (g3,) = steps("pass", pass_body, [g3], [narrow(size, feats)], after=[g1])
    g2 = swap(g3, "tok", 1)
    (send2,) = steps("send_far", send_body, [in_basis], [narrow(size, cols)], where=[far, most], **options)
    got2 = swap(send2, "tok", 1)
    (pair1,) = steps("pair_near", pair_body, [in_basis, got1], [narrow(size, cols)], where=[acts, pltpu.with_memory_space_constraint(near, pltpu.HBM)], **options)
    got1 = swap(pair1, "tok", 2)
    (out_basis,) = loaded("load_out", out_basis)
    mine_top, mine_low, top, low = steps(
        "rotate", rotate_body, [grads, g1, g3, g2, out_basis], [wide(size, depth)] * 2 + [narrow(size, depth)] * 2,
        scalars=scalars(tok, tok ^ 1, tok ^ 2, tok ^ 3, core),
        scratch=[pltpu.VMEM((4 * size, feats), NARROW)], flops=8 * size * feats * depth,
    )
    (pair2,) = steps("pair_far", pair_body, [in_basis, got2], [narrow(size, cols)], where=[far, most], **options)
    got2 = swap(pair2, "tok", 2)
    chips = [[2 * k, 2 * k + 1] for k in range(2)]

    def chip_sum(name, mine, other, *handed):
        both = lax.all_gather(other, "panel", axis=0, tiled=True, axis_index_groups=chips)
        mine, other, *handed = steps(
            name, chip_sum_body, [mine, both, *handed],
            [wide(size, depth), narrow(size, depth)] + [narrow(size, depth)] * len(handed), scalars=scalars(core),
        )
        return mine, swap(other, "panel", 2), *handed

    mine_top, top, low = chip_sum("chip_sum_top", mine_top, top, low)
    (total1,) = steps("total_near", add_body, [pair1, got1], [narrow(size, cols)])
    back1 = swap(total1, "tok", 1)
    mine_low, low = chip_sum("chip_sum_low", mine_low, low)
    (total2,) = steps("total_far", add_body, [pair2, got2], [narrow(size, cols)])
    back2 = swap(total2, "tok", 1)
    (mine_top,) = steps("panel_sum_top", panel_sum_body, [mine_top, top], [narrow(size, depth)], weight=8_000_000)
    other_top = swap(mine_top, "panel", 1)
    (mine_low,) = steps("panel_sum_low", panel_sum_body, [mine_low, low], [narrow(size, depth)])
    other_low = swap(mine_low, "panel", 1)
    steps("mark", mark_body, [], [wide(8, LANES)], after=[back1, back2])
    owners = lax.axis_size("panel") * lax.axis_size("tok")
    (partial,) = steps(
        "scores", score_body, [total1, back1, total2, back2, mine_top, mine_low, other_top, other_low],
        [wide(owners, queries, LANES)],
        scalars=scalars(panel ^ turn, panel ^ turn ^ 1, panel ^ turn ^ 2, panel ^ turn ^ 3, core),
        scratch=[
            pltpu.VMEM((4 * size, cols), NARROW),
            pltpu.VMEM((4 * size, depth), NARROW),
            pltpu.VMEM((SLOTS, LANES, queries, cols), NARROW),
            pltpu.VMEM((SLOTS, LANES, cols), WIDE),
            pltpu.SemaphoreType.DMA((SLOTS, 2)),
        ],
        room=28 * 1024 * 1024, flops=8 * size * depth * queries * cols, streamed=[query_rot, eigvals],
    )
    got = lax.all_to_all(partial, ("panel", "tok"), split_axis=0, concat_axis=0, tiled=True)
    (out,) = steps("final", final_body, [got], [wide(queries, 4 * size // owners)])
    return out.T


def any_score_kernel(query_ref, eig_ref, act_ref, grad_ref, out_ref, act_turned, grad_turned):
    step = pl.program_id(0)
    block, queries, cols = query_ref.shape
    tokens = out_ref.shape[1]
    piece = math.gcd(block, 32)

    @pl.when(step == 0)
    def _():
        act_turned[...] = act_ref[...].astype(WIDE).T.astype(NARROW)
        grad_turned[...] = grad_ref[...].astype(WIDE).T
        out_ref[...] = jnp.zeros_like(out_ref)

    total = out_ref[...]
    for k in range(block // piece):
        scale = 1.0 / (eig_ref[k * piece : (k + 1) * piece, :] + DAMPING)
        query = query_ref[k * piece : (k + 1) * piece].astype(WIDE) * scale[:, None, :]
        precond = query.reshape(piece * queries, cols).astype(NARROW)
        mixed = dot(precond, act_turned[...]).reshape(piece, queries, tokens)
        grad = grad_turned[pl.ds(pl.multiple_of(step * block + k * piece, piece), piece), :]
        total = total + jnp.sum(mixed * grad[:, None, :], axis=0)
    out_ref[...] = total


def on_any(grads, acts, out_basis, in_basis, query_rot, eigvals):
    acts_all = lax.all_gather(acts, "panel", axis=0, tiled=True)
    grads_all = lax.all_gather(grads, "tok", axis=0, tiled=True)
    act_rot = lax.psum(dot(acts_all, in_basis), "tok").astype(NARROW)
    grad_rot = lax.psum(dot(grads_all, out_basis), "panel").astype(NARROW)
    depth, queries, cols = query_rot.shape
    tokens = act_rot.shape[0]
    step = math.gcd(depth, 256)
    partial = pl.pallas_call(
        any_score_kernel,
        grid=(depth // step,),
        in_specs=[
            pl.BlockSpec((step, queries, cols), lambda i: (i, 0, 0)),
            pl.BlockSpec((step, cols), lambda i: (i, 0)),
            IN_VMEM,
            IN_VMEM,
        ],
        out_specs=pl.BlockSpec((queries, tokens), lambda i: (0, 0)),
        out_shape=jax.ShapeDtypeStruct((queries, tokens), WIDE),
        scratch_shapes=[pltpu.VMEM((cols, tokens), NARROW), pltpu.VMEM((depth, tokens), WIDE)],
        compiler_params=pltpu.CompilerParams(vmem_limit_bytes=ROOM),
        name="any_scores",
    )(query_rot, eigvals, act_rot, grad_rot)
    return jnp.sum(spread_out(partial), axis=0).T


def per_device(*arrays):
    four = lax.axis_size("panel") == 4 and lax.axis_size("tok") == 4
    return (on_lines_of_four if four else on_any)(*arrays)


def solution(mesh):
    placed = (
        P(("groups", "tok"), "panel"),
        P(("groups", "panel"), "tok"),
        P("panel", "tok"),
        P("tok", "panel"),
        P("tok", None, "panel"),
        P("tok", "panel"),
    )
    return jax.shard_map(
        per_device,
        mesh=mesh,
        in_specs=placed,
        out_specs=P(("groups", "panel", "tok"), None),
        check_vma=False,
    )
```

```python
import functools
import math

import jax
import jax.numpy as jnp
from jax import lax
from jax.experimental import pallas as pl
from jax.experimental.pallas import tpu as pltpu
from jax.sharding import PartitionSpec as P

DAMPING = 0.1
WIDE = jnp.float32
NARROW = jnp.bfloat16
ROOM = 48 * 1024 * 1024
LANES = 128
SLOTS = 3
KEPT = 1 << 19
IN_VMEM = pl.BlockSpec(memory_space=pltpu.VMEM)
IN_SMEM = pl.BlockSpec(memory_space=pltpu.SMEM)
ANYWHERE = pl.BlockSpec(memory_space=pl.ANY)


def swap(value, axis, mask):
    return lax.ppermute(value, axis, [(i, i ^ mask) for i in range(lax.axis_size(axis))])


def dot(a, b):
    return jnp.dot(a, b, preferred_element_type=WIDE)


class Steps:
    def __init__(self):
        self.last = None

    def __call__(self, name, body, ins, outs, scalars=None, scratch=(), room=16 * 1024 * 1024, flops=0, streamed=(), where=(), after=(), weight=0):
        def block(x):
            if math.prod(x.shape) > KEPT:
                return IN_VMEM
            return pl.BlockSpec(x.shape, lambda i: (0,) * len(x.shape))

        def home(x):
            if math.prod(x.shape) > KEPT:
                return pltpu.with_memory_space_constraint(x, pltpu.VMEM)
            return x

        def result(x):
            if math.prod(x.shape) > KEPT:
                return pltpu.VMEM(x.shape, x.dtype)
            return x

        streamed = [pltpu.with_memory_space_constraint(x, pltpu.HBM) for x in streamed]
        specs, args = [], []
        if scalars is not None:
            specs.append(IN_SMEM)
            args.append(scalars)
        specs += [block(x) for x in ins] + [ANYWHERE] * (len(streamed) + len(where))
        args += [home(x) for x in ins] + streamed + list(where)
        kept = len(args)
        ties = list(after) + ([] if self.last is None else [self.last])
        specs += [ANYWHERE] * len(ties)
        args += ties
        given = len(args)

        def kernel(*refs):
            body(*refs[:kept], *refs[given:])

        moved = weight + sum(math.prod(x.shape) * x.dtype.itemsize for x in [*ins, *outs, *streamed])
        results = pl.pallas_call(
            kernel,
            grid=(1,),
            in_specs=specs,
            out_specs=[block(x) for x in outs],
            out_shape=[result(x) for x in outs],
            scratch_shapes=list(scratch),
            compiler_params=pltpu.CompilerParams(vmem_limit_bytes=room),
            cost_estimate=pl.CostEstimate(flops=flops, bytes_accessed=moved, transcendentals=0),
            name=name,
        )(*args)
        self.last = results[-1]
        return results


def load_body(*refs):
    count = len(refs) // 2
    sems = refs[-1]
    copies = [pltpu.make_async_copy(refs[k], refs[count + k], sems.at[k]) for k in range(count)]
    for copy in copies:
        copy.start()
    for copy in copies:
        copy.wait()


def load_send_body(turn_ref, basis_ref, a_ref, b_ref, held, send_ref, rows_ref, sem, sems):
    blocks = fetch(basis_ref, held, sems)
    pick(turn_ref[0], b_ref, a_ref, rows_ref, sem)
    total = None
    for rows, copy in blocks:
        copy.wait()
        value = dot(rows_ref[:, rows], held[rows, :])
        total = value if total is None else total + value
    send_ref[...] = total.astype(NARROW)


def fetch(source, held, sems):
    count = sems.shape[0]
    size = source.shape[0] // count
    found = []
    for k in range(count):
        rows = pl.ds(k * size, size)
        copy = pltpu.make_async_copy(source.at[rows], held.at[rows], sems.at[k])
        copy.start()
        found.append((rows, copy))
    return found


def send_body(turn_ref, basis_ref, a_ref, b_ref, send_ref, rows_ref, sem):
    pick(turn_ref[0], b_ref, a_ref, rows_ref, sem)
    send_ref[...] = dot(rows_ref[...], basis_ref[...]).astype(NARROW)


def pick(turn, zero_ref, one_ref, rows_ref, sem):
    @pl.when(turn == 0)
    def _():
        copy = pltpu.make_async_copy(zero_ref, rows_ref, sem)
        copy.start()
        copy.wait()

    @pl.when(turn == 1)
    def _():
        copy = pltpu.make_async_copy(one_ref, rows_ref, sem)
        copy.start()
        copy.wait()


def pair_body(turn_ref, basis_ref, got_ref, a_ref, b_ref, out_ref, rows_ref, sem):
    pick(turn_ref[0], a_ref, b_ref, rows_ref, sem)
    out_ref[...] = (dot(rows_ref[...], basis_ref[...]) + got_ref[...].astype(WIDE)).astype(NARROW)


def pass_body(a_ref, out_ref):
    out_ref[...] = a_ref[...]


def mark_body(out_ref):
    out_ref[...] = jnp.zeros_like(out_ref)


def add_body(a_ref, b_ref, out_ref):
    out_ref[...] = (a_ref[...].astype(WIDE) + b_ref[...].astype(WIDE)).astype(NARROW)


def rotate_body(place_ref, b0, b1, b2, b3, basis_ref, mine_top, mine_low, top_ref, low_ref, rows_ref):
    size = b0.shape[0]
    half = 2 * size
    for k, block in enumerate((b0, b1, b2, b3)):
        rows_ref[pl.ds(pl.multiple_of(place_ref[k] * size, size), size), :] = block[...]
    core = place_ref[4]
    other = dot(rows_ref[pl.ds(pl.multiple_of((1 - core) * half, half), half), :], basis_ref[...])
    top_ref[...] = other[:size].astype(NARROW)
    low_ref[...] = other[size:].astype(NARROW)
    mine = dot(rows_ref[pl.ds(pl.multiple_of(core * half, half), half), :], basis_ref[...])
    mine_top[...] = mine[:size]
    mine_low[...] = mine[size:]


def chip_sum_body(core_ref, mine_ref, pair_ref, *refs):
    given = (len(refs) - 2) // 2
    wide_ref, out_ref = refs[given], refs[given + 1]
    size = out_ref.shape[0]
    source = pl.ds(pl.multiple_of((1 - core_ref[0]) * size, size), size)
    value = mine_ref[...] + pair_ref[source, :].astype(WIDE)
    wide_ref[...] = value
    out_ref[...] = value.astype(NARROW)
    for k in range(given):
        refs[given + 2 + k][...] = refs[k][...]


def panel_sum_body(wide_ref, got_ref, out_ref):
    out_ref[...] = (wide_ref[...] + got_ref[...].astype(WIDE)).astype(NARROW)


def score_body(
    spot_ref, a0, a1, a2, a3, mine_top, mine_low, other_top, other_low, query_ref, eig_ref, out_ref,
    act_ref, grad_ref, query_buf, eig_buf, sems
):
    depth, queries, cols = query_ref.shape
    owners = out_ref.shape[0]
    tokens = 4 * a0.shape[0]
    count = depth // LANES

    def copies(k):
        slot = lax.rem(k, SLOTS)
        rows = pl.ds(pl.multiple_of(k * LANES, LANES), LANES)
        return (
            pltpu.make_async_copy(query_ref.at[rows], query_buf.at[slot], sems.at[slot, 0]),
            pltpu.make_async_copy(eig_ref.at[rows], eig_buf.at[slot], sems.at[slot, 1]),
        )

    for k in range(SLOTS - 1):
        for copy in copies(k):
            copy.start()

    size = tokens // 4
    for k, block in enumerate((a0, a1, a2, a3)):
        act_ref[pl.ds(pl.multiple_of(spot_ref[k] * size, size), size), :] = block[...]
    core = spot_ref[4]
    for first, refs in ((core, (mine_top, mine_low)), (1 - core, (other_top, other_low))):
        for k, ref in enumerate(refs):
            grad_ref[pl.ds(pl.multiple_of((2 * first + k) * size, size), size), :] = ref[...]

    group = LANES // queries
    lane = lax.broadcasted_iota(jnp.int32, (tokens, LANES), 1) // queries

    def step(k, total):
        @pl.when(k + SLOTS - 1 < count)
        def _():
            for copy in copies(k + SLOTS - 1):
                copy.start()

        for copy in copies(k):
            copy.wait()
        slot = lax.rem(k, SLOTS)
        start = pl.multiple_of(k * LANES, LANES)
        scale = 1.0 / (eig_buf[slot] + DAMPING)
        query = query_buf[slot].astype(WIDE) * scale[:, None, :]
        precond = query.reshape(LANES * queries, cols).astype(NARROW)
        mixed = lax.dot_general(
            act_ref[...], precond, (((1,), (1,)), ((), ())), preferred_element_type=WIDE
        )
        grad = grad_ref[:, pl.ds(start, LANES)].astype(WIDE)
        for part in range(queries):
            spread = jnp.take_along_axis(grad, lane + part * group, axis=1)
            total = total + mixed[:, part * LANES : (part + 1) * LANES] * spread
        return total

    total = lax.fori_loop(0, count, step, jnp.zeros((tokens, LANES), WIDE))
    shift = LANES // 2
    while shift >= queries:
        total = total + pltpu.roll(total, shift, 1)
        shift //= 2
    turned = total.T[:queries, :]
    owned = tokens // owners
    for k in range(owners):
        out_ref[k, :, :owned] = turned[:, k * owned : (k + 1) * owned]


def final_body(got_ref, out_ref):
    out_ref[...] = jnp.sum(got_ref[...], axis=0)[:, : out_ref.shape[1]]


def spread_out(partial):
    queries, tokens = partial.shape
    owners = lax.axis_size("panel") * lax.axis_size("tok")
    split = partial.reshape(queries, owners, tokens // owners).transpose(1, 0, 2)
    return lax.all_to_all(split, ("panel", "tok"), split_axis=0, concat_axis=0, tiled=True)


def on_lines_of_four(grads, acts, out_basis, in_basis, query_rot, eigvals):
    size, feats = grads.shape
    depth, queries, cols = query_rot.shape
    panel, tok = lax.axis_index("panel"), lax.axis_index("tok")
    core, turn = panel % 2, (tok ^ tok // 2) % 2
    steps = Steps()

    def wide(*shape):
        return jax.ShapeDtypeStruct(shape, WIDE)

    def narrow(*shape):
        return jax.ShapeDtypeStruct(shape, NARROW)

    def scalars(*values):
        return jnp.stack(values).astype(jnp.int32)

    g1, g3 = swap(grads, "tok", 1), swap(grads, "tok", 2)
    near = swap(acts, "panel", 1)
    far = swap(acts, "panel", 2)
    most = swap(acts, "panel", 3)

    def loaded(name, *arrays):
        return steps(
            name, load_body, [], [narrow(*x.shape) for x in arrays],
            scratch=[pltpu.SemaphoreType.DMA((len(arrays),))], streamed=arrays,
        )

    one = [pltpu.VMEM((size, feats), NARROW), pltpu.SemaphoreType.DMA]
    cost = 2 * size * feats * cols
    options = dict(scalars=scalars(turn), scratch=one, flops=cost)
    acts = pltpu.with_memory_space_constraint(acts, pltpu.HBM)
    in_basis, send1 = steps(
        "send_near", load_send_body, [], [narrow(*in_basis.shape), narrow(size, cols)], scalars=scalars(turn),
        scratch=one + [pltpu.SemaphoreType.DMA((4,))], flops=cost, streamed=[in_basis], where=[acts, pltpu.with_memory_space_constraint(near, pltpu.HBM)],
    )
    got1 = swap(send1, "tok", 1)
    (g3,) = steps("pass", pass_body, [g3], [narrow(size, feats)], after=[g1])
    g2 = swap(g3, "tok", 1)
    (send2,) = steps("send_far", send_body, [in_basis], [narrow(size, cols)], where=[far, most], **options)
    got2 = swap(send2, "tok", 1)
    (pair1,) = steps("pair_near", pair_body, [in_basis, got1], [narrow(size, cols)], where=[acts, pltpu.with_memory_space_constraint(near, pltpu.HBM)], **options)
    got1 = swap(pair1, "tok", 3)
    (out_basis,) = loaded("load_out", out_basis)
    mine_top, mine_low, top, low = steps(
        "rotate", rotate_body, [grads, g1, g3, g2, out_basis], [wide(size, depth)] * 2 + [narrow(size, depth)] * 2,
        scalars=scalars(tok, tok ^ 1, tok ^ 2, tok ^ 3, core),
        scratch=[pltpu.VMEM((4 * size, feats), NARROW)], flops=8 * size * feats * depth,
    )
    chips = [[2 * k, 2 * k + 1] for k in range(2)]

    def chip_sum(name, mine, other, *handed):
        both = lax.all_gather(other, "panel", axis=0, tiled=True, axis_index_groups=chips)
        mine, other, *handed = steps(
            name, chip_sum_body, [mine, both, *handed],
            [wide(size, depth), narrow(size, depth)] + [narrow(size, depth)] * len(handed), scalars=scalars(core),
        )
        return mine, swap(other, "panel", 2), *handed

    mine_top, top, low = chip_sum("chip_sum_top", mine_top, top, low)
    (pair2,) = steps("pair_far", pair_body, [in_basis, got2], [narrow(size, cols)], where=[far, most], **options)
    got2 = swap(pair2, "tok", 3)
    (total1,) = steps("total_near", add_body, [pair1, got1], [narrow(size, cols)])
    back1 = swap(total1, "tok", 1)
    mine_low, low = chip_sum("chip_sum_low", mine_low, low)
    (total2,) = steps("total_far", add_body, [pair2, got2], [narrow(size, cols)])
    back2 = swap(total2, "tok", 1)
    steps("mark_near", mark_body, [], [wide(8, LANES)], after=[back1])
    (mine_top,) = steps("panel_sum_top", panel_sum_body, [mine_top, top], [narrow(size, depth)], weight=8_000_000)
    other_top = swap(mine_top, "panel", 1)
    (mine_low,) = steps("panel_sum_low", panel_sum_body, [mine_low, low], [narrow(size, depth)])
    other_low = swap(mine_low, "panel", 1)
    steps("mark_far", mark_body, [], [wide(8, LANES)], after=[back2])
    owners = lax.axis_size("panel") * lax.axis_size("tok")
    (partial,) = steps(
        "scores", score_body, [total1, back1, total2, back2, mine_top, mine_low, other_top, other_low],
        [wide(owners, queries, LANES)],
        scalars=scalars(panel ^ turn, panel ^ turn ^ 1, panel ^ turn ^ 2, panel ^ turn ^ 3, core),
        scratch=[
            pltpu.VMEM((4 * size, cols), NARROW),
            pltpu.VMEM((4 * size, depth), NARROW),
            pltpu.VMEM((SLOTS, LANES, queries, cols), NARROW),
            pltpu.VMEM((SLOTS, LANES, cols), WIDE),
            pltpu.SemaphoreType.DMA((SLOTS, 2)),
        ],
        room=28 * 1024 * 1024, flops=8 * size * depth * queries * cols, streamed=[query_rot, eigvals],
    )
    got = lax.all_to_all(partial, ("panel", "tok"), split_axis=0, concat_axis=0, tiled=True)
    (out,) = steps("final", final_body, [got], [wide(queries, 4 * size // owners)])
    return out.T


def any_score_kernel(query_ref, eig_ref, act_ref, grad_ref, out_ref, act_turned, grad_turned):
    step = pl.program_id(0)
    block, queries, cols = query_ref.shape
    tokens = out_ref.shape[1]
    piece = math.gcd(block, 32)

    @pl.when(step == 0)
    def _():
        act_turned[...] = act_ref[...].astype(WIDE).T.astype(NARROW)
        grad_turned[...] = grad_ref[...].astype(WIDE).T
        out_ref[...] = jnp.zeros_like(out_ref)

    total = out_ref[...]
    for k in range(block // piece):
        scale = 1.0 / (eig_ref[k * piece : (k + 1) * piece, :] + DAMPING)
        query = query_ref[k * piece : (k + 1) * piece].astype(WIDE) * scale[:, None, :]
        precond = query.reshape(piece * queries, cols).astype(NARROW)
        mixed = dot(precond, act_turned[...]).reshape(piece, queries, tokens)
        grad = grad_turned[pl.ds(pl.multiple_of(step * block + k * piece, piece), piece), :]
        total = total + jnp.sum(mixed * grad[:, None, :], axis=0)
    out_ref[...] = total


def on_any(grads, acts, out_basis, in_basis, query_rot, eigvals):
    acts_all = lax.all_gather(acts, "panel", axis=0, tiled=True)
    grads_all = lax.all_gather(grads, "tok", axis=0, tiled=True)
    act_rot = lax.psum(dot(acts_all, in_basis), "tok").astype(NARROW)
    grad_rot = lax.psum(dot(grads_all, out_basis), "panel").astype(NARROW)
    depth, queries, cols = query_rot.shape
    tokens = act_rot.shape[0]
    step = math.gcd(depth, 256)
    partial = pl.pallas_call(
        any_score_kernel,
        grid=(depth // step,),
        in_specs=[
            pl.BlockSpec((step, queries, cols), lambda i: (i, 0, 0)),
            pl.BlockSpec((step, cols), lambda i: (i, 0)),
            IN_VMEM,
            IN_VMEM,
        ],
        out_specs=pl.BlockSpec((queries, tokens), lambda i: (0, 0)),
        out_shape=jax.ShapeDtypeStruct((queries, tokens), WIDE),
        scratch_shapes=[pltpu.VMEM((cols, tokens), NARROW), pltpu.VMEM((depth, tokens), WIDE)],
        compiler_params=pltpu.CompilerParams(vmem_limit_bytes=ROOM),
        name="any_scores",
    )(query_rot, eigvals, act_rot, grad_rot)
    return jnp.sum(spread_out(partial), axis=0).T


def per_device(*arrays):
    four = lax.axis_size("panel") == 4 and lax.axis_size("tok") == 4
    return (on_lines_of_four if four else on_any)(*arrays)


def solution(mesh):
    placed = (
        P(("groups", "tok"), "panel"),
        P(("groups", "panel"), "tok"),
        P("panel", "tok"),
        P("tok", "panel"),
        P("tok", None, "panel"),
        P("tok", "panel"),
    )
    return jax.shard_map(
        per_device,
        mesh=mesh,
        in_specs=placed,
        out_specs=P(("groups", "panel", "tok"), None),
        check_vma=False,
    )
```

```python
import functools
import math

import jax
import jax.numpy as jnp
from jax import lax
from jax.experimental import pallas as pl
from jax.experimental.pallas import tpu as pltpu
from jax.sharding import PartitionSpec as P

DAMPING = 0.1
WIDE = jnp.float32
NARROW = jnp.bfloat16
ROOM = 48 * 1024 * 1024
LANES = 128
SLOTS = 3
KEPT = 1 << 19
IN_VMEM = pl.BlockSpec(memory_space=pltpu.VMEM)
IN_SMEM = pl.BlockSpec(memory_space=pltpu.SMEM)
ANYWHERE = pl.BlockSpec(memory_space=pl.ANY)


def swap(value, axis, mask):
    return lax.ppermute(value, axis, [(i, i ^ mask) for i in range(lax.axis_size(axis))])


def dot(a, b):
    return jnp.dot(a, b, preferred_element_type=WIDE)


class Steps:
    def __init__(self):
        self.last = None

    def __call__(self, name, body, ins, outs, scalars=None, scratch=(), room=16 * 1024 * 1024, flops=0, streamed=(), where=(), after=(), weight=0):
        def block(x):
            if math.prod(x.shape) > KEPT:
                return IN_VMEM
            return pl.BlockSpec(x.shape, lambda i: (0,) * len(x.shape))

        def home(x):
            if math.prod(x.shape) > KEPT:
                return pltpu.with_memory_space_constraint(x, pltpu.VMEM)
            return x

        def result(x):
            if math.prod(x.shape) > KEPT:
                return pltpu.VMEM(x.shape, x.dtype)
            return x

        streamed = [pltpu.with_memory_space_constraint(x, pltpu.HBM) for x in streamed]
        specs, args = [], []
        if scalars is not None:
            specs.append(IN_SMEM)
            args.append(scalars)
        specs += [block(x) for x in ins] + [ANYWHERE] * (len(streamed) + len(where))
        args += [home(x) for x in ins] + streamed + list(where)
        kept = len(args)
        ties = list(after) + ([] if self.last is None else [self.last])
        specs += [ANYWHERE] * len(ties)
        args += ties
        given = len(args)

        def kernel(*refs):
            body(*refs[:kept], *refs[given:])

        moved = weight + sum(math.prod(x.shape) * x.dtype.itemsize for x in [*ins, *outs, *streamed])
        results = pl.pallas_call(
            kernel,
            grid=(1,),
            in_specs=specs,
            out_specs=[block(x) for x in outs],
            out_shape=[result(x) for x in outs],
            scratch_shapes=list(scratch),
            compiler_params=pltpu.CompilerParams(vmem_limit_bytes=room),
            cost_estimate=pl.CostEstimate(flops=flops, bytes_accessed=moved, transcendentals=0),
            name=name,
        )(*args)
        self.last = results[-1]
        return results


def load_body(*refs):
    count = len(refs) // 2
    sems = refs[-1]
    copies = [pltpu.make_async_copy(refs[k], refs[count + k], sems.at[k]) for k in range(count)]
    for copy in copies:
        copy.start()
    for copy in copies:
        copy.wait()


def load_send_body(turn_ref, basis_ref, a_ref, b_ref, held, send_ref, rows_ref, sem, sems):
    blocks = fetch(basis_ref, held, sems)
    pick(turn_ref[0], b_ref, a_ref, rows_ref, sem)
    total = None
    for rows, copy in blocks:
        copy.wait()
        value = dot(rows_ref[:, rows], held[rows, :])
        total = value if total is None else total + value
    send_ref[...] = total.astype(NARROW)


def fetch(source, held, sems):
    count = sems.shape[0]
    size = source.shape[0] // count
    found = []
    for k in range(count):
        rows = pl.ds(k * size, size)
        copy = pltpu.make_async_copy(source.at[rows], held.at[rows], sems.at[k])
        copy.start()
        found.append((rows, copy))
    return found


def send_body(turn_ref, basis_ref, a_ref, b_ref, send_ref, rows_ref, sem):
    pick(turn_ref[0], b_ref, a_ref, rows_ref, sem)
    send_ref[...] = dot(rows_ref[...], basis_ref[...]).astype(NARROW)


def pick(turn, zero_ref, one_ref, rows_ref, sem):
    @pl.when(turn == 0)
    def _():
        copy = pltpu.make_async_copy(zero_ref, rows_ref, sem)
        copy.start()
        copy.wait()

    @pl.when(turn == 1)
    def _():
        copy = pltpu.make_async_copy(one_ref, rows_ref, sem)
        copy.start()
        copy.wait()


def pair_body(turn_ref, basis_ref, got_ref, a_ref, b_ref, out_ref, rows_ref, sem):
    pick(turn_ref[0], a_ref, b_ref, rows_ref, sem)
    out_ref[...] = (dot(rows_ref[...], basis_ref[...]) + got_ref[...].astype(WIDE)).astype(NARROW)


def pass_body(a_ref, out_ref):
    out_ref[...] = a_ref[...]


def mark_body(out_ref):
    out_ref[...] = jnp.zeros_like(out_ref)


def add_body(a_ref, b_ref, out_ref):
    out_ref[...] = (a_ref[...].astype(WIDE) + b_ref[...].astype(WIDE)).astype(NARROW)


def rotate_body(place_ref, b0, b1, b2, b3, basis_ref, mine_top, mine_low, top_ref, low_ref, rows_ref):
    size = b0.shape[0]
    half = 2 * size
    for k, block in enumerate((b0, b1, b2, b3)):
        rows_ref[pl.ds(pl.multiple_of(place_ref[k] * size, size), size), :] = block[...]
    core = place_ref[4]
    other = dot(rows_ref[pl.ds(pl.multiple_of((1 - core) * half, half), half), :], basis_ref[...])
    top_ref[...] = other[:size].astype(NARROW)
    low_ref[...] = other[size:].astype(NARROW)
    mine = dot(rows_ref[pl.ds(pl.multiple_of(core * half, half), half), :], basis_ref[...])
    mine_top[...] = mine[:size]
    mine_low[...] = mine[size:]


def chip_sum_body(core_ref, mine_ref, pair_ref, *refs):
    given = (len(refs) - 2) // 2
    wide_ref, out_ref = refs[given], refs[given + 1]
    size = out_ref.shape[0]
    source = pl.ds(pl.multiple_of((1 - core_ref[0]) * size, size), size)
    value = mine_ref[...] + pair_ref[source, :].astype(WIDE)
    wide_ref[...] = value
    out_ref[...] = value.astype(NARROW)
    for k in range(given):
        refs[given + 2 + k][...] = refs[k][...]


def panel_sum_body(wide_ref, got_ref, out_ref):
    out_ref[...] = (wide_ref[...] + got_ref[...].astype(WIDE)).astype(NARROW)


def score_body(
    spot_ref, a0, a1, a2, a3, mine_top, mine_low, other_top, other_low, query_ref, eig_ref, out_ref,
    act_ref, grad_ref, query_buf, eig_buf, sems
):
    depth, queries, cols = query_ref.shape
    owners = out_ref.shape[0]
    tokens = 4 * a0.shape[0]
    count = depth // LANES

    def copies(k):
        slot = lax.rem(k, SLOTS)
        rows = pl.ds(pl.multiple_of(k * LANES, LANES), LANES)
        return (
            pltpu.make_async_copy(query_ref.at[rows], query_buf.at[slot], sems.at[slot, 0]),
            pltpu.make_async_copy(eig_ref.at[rows], eig_buf.at[slot], sems.at[slot, 1]),
        )

    for k in range(SLOTS - 1):
        for copy in copies(k):
            copy.start()

    size = tokens // 4
    for k, block in enumerate((a0, a1, a2, a3)):
        act_ref[pl.ds(pl.multiple_of(spot_ref[k] * size, size), size), :] = block[...]
    core = spot_ref[4]
    for first, refs in ((core, (mine_top, mine_low)), (1 - core, (other_top, other_low))):
        for k, ref in enumerate(refs):
            grad_ref[pl.ds(pl.multiple_of((2 * first + k) * size, size), size), :] = ref[...]

    group = LANES // queries
    lane = lax.broadcasted_iota(jnp.int32, (tokens, LANES), 1) // queries

    def step(k, total):
        @pl.when(k + SLOTS - 1 < count)
        def _():
            for copy in copies(k + SLOTS - 1):
                copy.start()

        for copy in copies(k):
            copy.wait()
        slot = lax.rem(k, SLOTS)
        start = pl.multiple_of(k * LANES, LANES)
        scale = 1.0 / (eig_buf[slot] + DAMPING)
        query = query_buf[slot].astype(WIDE) * scale[:, None, :]
        precond = query.reshape(LANES * queries, cols).astype(NARROW)
        mixed = lax.dot_general(
            act_ref[...], precond, (((1,), (1,)), ((), ())), preferred_element_type=WIDE
        )
        grad = grad_ref[:, pl.ds(start, LANES)].astype(WIDE)
        for part in range(queries):
            spread = jnp.take_along_axis(grad, lane + part * group, axis=1)
            total = total + mixed[:, part * LANES : (part + 1) * LANES] * spread
        return total

    total = lax.fori_loop(0, count, step, jnp.zeros((tokens, LANES), WIDE))
    shift = LANES // 2
    while shift >= queries:
        total = total + pltpu.roll(total, shift, 1)
        shift //= 2
    turned = total.T[:queries, :]
    owned = tokens // owners
    for k in range(owners):
        out_ref[k, :, :owned] = turned[:, k * owned : (k + 1) * owned]


def final_body(got_ref, out_ref):
    out_ref[...] = jnp.sum(got_ref[...], axis=0)[:, : out_ref.shape[1]]


def spread_out(partial):
    queries, tokens = partial.shape
    owners = lax.axis_size("panel") * lax.axis_size("tok")
    split = partial.reshape(queries, owners, tokens // owners).transpose(1, 0, 2)
    return lax.all_to_all(split, ("panel", "tok"), split_axis=0, concat_axis=0, tiled=True)


def on_lines_of_four(grads, acts, out_basis, in_basis, query_rot, eigvals):
    size, feats = grads.shape
    depth, queries, cols = query_rot.shape
    panel, tok = lax.axis_index("panel"), lax.axis_index("tok")
    core, turn = panel % 2, (tok ^ tok // 2) % 2
    steps = Steps()

    def wide(*shape):
        return jax.ShapeDtypeStruct(shape, WIDE)

    def narrow(*shape):
        return jax.ShapeDtypeStruct(shape, NARROW)

    def scalars(*values):
        return jnp.stack(values).astype(jnp.int32)

    g1, g3 = swap(grads, "tok", 1), swap(grads, "tok", 2)
    near = swap(acts, "panel", 1)
    far = swap(acts, "panel", 2)
    most = swap(acts, "panel", 3)

    def loaded(name, *arrays):
        return steps(
            name, load_body, [], [narrow(*x.shape) for x in arrays],
            scratch=[pltpu.SemaphoreType.DMA((len(arrays),))], streamed=arrays,
        )

    one = [pltpu.VMEM((size, feats), NARROW), pltpu.SemaphoreType.DMA]
    cost = 2 * size * feats * cols
    options = dict(scalars=scalars(turn), scratch=one, flops=cost)
    acts = pltpu.with_memory_space_constraint(acts, pltpu.HBM)
    in_basis, send1 = steps(
        "send_near", load_send_body, [], [narrow(*in_basis.shape), narrow(size, cols)], scalars=scalars(turn),
        scratch=one + [pltpu.SemaphoreType.DMA((4,))], flops=cost, streamed=[in_basis], where=[acts, pltpu.with_memory_space_constraint(near, pltpu.HBM)],
    )
    got1 = swap(send1, "tok", 1)
    (g3,) = steps("pass", pass_body, [g3], [narrow(size, feats)], after=[g1])
    g2 = swap(g3, "tok", 1)
    (send2,) = steps("send_far", send_body, [in_basis], [narrow(size, cols)], where=[far, most], **options)
    got2 = swap(send2, "tok", 1)
    (pair1,) = steps("pair_near", pair_body, [in_basis, got1], [narrow(size, cols)], where=[acts, pltpu.with_memory_space_constraint(near, pltpu.HBM)], **options)
    got1 = swap(pair1, "tok", 3)
    (out_basis,) = loaded("load_out", out_basis)
    mine_top, mine_low, top, low = steps(
        "rotate", rotate_body, [grads, g1, g3, g2, out_basis], [wide(size, depth)] * 2 + [narrow(size, depth)] * 2,
        scalars=scalars(tok, tok ^ 1, tok ^ 2, tok ^ 3, core),
        scratch=[pltpu.VMEM((4 * size, feats), NARROW)], flops=8 * size * feats * depth,
    )
    chips = [[2 * k, 2 * k + 1] for k in range(2)]

    def chip_sum(name, mine, other, *handed):
        both = lax.all_gather(other, "panel", axis=0, tiled=True, axis_index_groups=chips)
        mine, other, *handed = steps(
            name, chip_sum_body, [mine, both, *handed],
            [wide(size, depth), narrow(size, depth)] + [narrow(size, depth)] * len(handed), scalars=scalars(core),
        )
        return mine, swap(other, "panel", 2), *handed

    mine_top, top, low = chip_sum("chip_sum_top", mine_top, top, low)
    (pair2,) = steps("pair_far", pair_body, [in_basis, got2], [narrow(size, cols)], where=[far, most], **options)
    got2 = swap(pair2, "tok", 3)
    mine_low, low = chip_sum("chip_sum_low", mine_low, low)
    (total1,) = steps("total_near", add_body, [pair1, got1], [narrow(size, cols)])
    back1 = swap(total1, "tok", 1)
    (total2,) = steps("total_far", add_body, [pair2, got2], [narrow(size, cols)])
    back2 = swap(total2, "tok", 1)
    steps("mark_near", mark_body, [], [wide(8, LANES)], after=[back1])
    (mine_top,) = steps("panel_sum_top", panel_sum_body, [mine_top, top], [narrow(size, depth)], weight=8_000_000)
    other_top = swap(mine_top, "panel", 1)
    (mine_low,) = steps("panel_sum_low", panel_sum_body, [mine_low, low], [narrow(size, depth)])
    other_low = swap(mine_low, "panel", 1)
    steps("mark_far", mark_body, [], [wide(8, LANES)], after=[back2])
    owners = lax.axis_size("panel") * lax.axis_size("tok")
    (partial,) = steps(
        "scores", score_body, [total1, back1, total2, back2, mine_top, mine_low, other_top, other_low],
        [wide(owners, queries, LANES)],
        scalars=scalars(panel ^ turn, panel ^ turn ^ 1, panel ^ turn ^ 2, panel ^ turn ^ 3, core),
        scratch=[
            pltpu.VMEM((4 * size, cols), NARROW),
            pltpu.VMEM((4 * size, depth), NARROW),
            pltpu.VMEM((SLOTS, LANES, queries, cols), NARROW),
            pltpu.VMEM((SLOTS, LANES, cols), WIDE),
            pltpu.SemaphoreType.DMA((SLOTS, 2)),
        ],
        room=28 * 1024 * 1024, flops=8 * size * depth * queries * cols, streamed=[query_rot, eigvals],
    )
    got = lax.all_to_all(partial, ("panel", "tok"), split_axis=0, concat_axis=0, tiled=True)
    (out,) = steps("final", final_body, [got], [wide(queries, 4 * size // owners)])
    return out.T


def any_score_kernel(query_ref, eig_ref, act_ref, grad_ref, out_ref, act_turned, grad_turned):
    step = pl.program_id(0)
    block, queries, cols = query_ref.shape
    tokens = out_ref.shape[1]
    piece = math.gcd(block, 32)

    @pl.when(step == 0)
    def _():
        act_turned[...] = act_ref[...].astype(WIDE).T.astype(NARROW)
        grad_turned[...] = grad_ref[...].astype(WIDE).T
        out_ref[...] = jnp.zeros_like(out_ref)

    total = out_ref[...]
    for k in range(block // piece):
        scale = 1.0 / (eig_ref[k * piece : (k + 1) * piece, :] + DAMPING)
        query = query_ref[k * piece : (k + 1) * piece].astype(WIDE) * scale[:, None, :]
        precond = query.reshape(piece * queries, cols).astype(NARROW)
        mixed = dot(precond, act_turned[...]).reshape(piece, queries, tokens)
        grad = grad_turned[pl.ds(pl.multiple_of(step * block + k * piece, piece), piece), :]
        total = total + jnp.sum(mixed * grad[:, None, :], axis=0)
    out_ref[...] = total


def on_any(grads, acts, out_basis, in_basis, query_rot, eigvals):
    acts_all = lax.all_gather(acts, "panel", axis=0, tiled=True)
    grads_all = lax.all_gather(grads, "tok", axis=0, tiled=True)
    act_rot = lax.psum(dot(acts_all, in_basis), "tok").astype(NARROW)
    grad_rot = lax.psum(dot(grads_all, out_basis), "panel").astype(NARROW)
    depth, queries, cols = query_rot.shape
    tokens = act_rot.shape[0]
    step = math.gcd(depth, 256)
    partial = pl.pallas_call(
        any_score_kernel,
        grid=(depth // step,),
        in_specs=[
            pl.BlockSpec((step, queries, cols), lambda i: (i, 0, 0)),
            pl.BlockSpec((step, cols), lambda i: (i, 0)),
            IN_VMEM,
            IN_VMEM,
        ],
        out_specs=pl.BlockSpec((queries, tokens), lambda i: (0, 0)),
        out_shape=jax.ShapeDtypeStruct((queries, tokens), WIDE),
        scratch_shapes=[pltpu.VMEM((cols, tokens), NARROW), pltpu.VMEM((depth, tokens), WIDE)],
        compiler_params=pltpu.CompilerParams(vmem_limit_bytes=ROOM),
        name="any_scores",
    )(query_rot, eigvals, act_rot, grad_rot)
    return jnp.sum(spread_out(partial), axis=0).T


def per_device(*arrays):
    four = lax.axis_size("panel") == 4 and lax.axis_size("tok") == 4
    return (on_lines_of_four if four else on_any)(*arrays)


def solution(mesh):
    placed = (
        P(("groups", "tok"), "panel"),
        P(("groups", "panel"), "tok"),
        P("panel", "tok"),
        P("tok", "panel"),
        P("tok", None, "panel"),
        P("tok", "panel"),
    )
    return jax.shard_map(
        per_device,
        mesh=mesh,
        in_specs=placed,
        out_specs=P(("groups", "panel", "tok"), None),
        check_vma=False,
    )
```

```python
import functools
import math

import jax
import jax.numpy as jnp
from jax import lax
from jax.experimental import pallas as pl
from jax.experimental.pallas import tpu as pltpu
from jax.sharding import PartitionSpec as P

DAMPING = 0.1
WIDE = jnp.float32
NARROW = jnp.bfloat16
ROOM = 48 * 1024 * 1024
LANES = 128
SLOTS = 3
KEPT = 1 << 19
IN_VMEM = pl.BlockSpec(memory_space=pltpu.VMEM)
IN_SMEM = pl.BlockSpec(memory_space=pltpu.SMEM)
ANYWHERE = pl.BlockSpec(memory_space=pl.ANY)


def swap(value, axis, mask):
    return lax.ppermute(value, axis, [(i, i ^ mask) for i in range(lax.axis_size(axis))])


def dot(a, b):
    return jnp.dot(a, b, preferred_element_type=WIDE)


class Steps:
    def __init__(self):
        self.last = None

    def __call__(self, name, body, ins, outs, scalars=None, scratch=(), room=16 * 1024 * 1024, flops=0, streamed=(), where=(), after=(), weight=0):
        def block(x):
            if math.prod(x.shape) > KEPT:
                return IN_VMEM
            return pl.BlockSpec(x.shape, lambda i: (0,) * len(x.shape))

        def home(x):
            if math.prod(x.shape) > KEPT:
                return pltpu.with_memory_space_constraint(x, pltpu.VMEM)
            return x

        def result(x):
            if math.prod(x.shape) > KEPT:
                return pltpu.VMEM(x.shape, x.dtype)
            return x

        streamed = [pltpu.with_memory_space_constraint(x, pltpu.HBM) for x in streamed]
        specs, args = [], []
        if scalars is not None:
            specs.append(IN_SMEM)
            args.append(scalars)
        specs += [block(x) for x in ins] + [ANYWHERE] * (len(streamed) + len(where))
        args += [home(x) for x in ins] + streamed + list(where)
        kept = len(args)
        ties = list(after) + ([] if self.last is None else [self.last])
        specs += [ANYWHERE] * len(ties)
        args += ties
        given = len(args)

        def kernel(*refs):
            body(*refs[:kept], *refs[given:])

        moved = weight + sum(math.prod(x.shape) * x.dtype.itemsize for x in [*ins, *outs, *streamed])
        results = pl.pallas_call(
            kernel,
            grid=(1,),
            in_specs=specs,
            out_specs=[block(x) for x in outs],
            out_shape=[result(x) for x in outs],
            scratch_shapes=list(scratch),
            compiler_params=pltpu.CompilerParams(vmem_limit_bytes=room),
            cost_estimate=pl.CostEstimate(flops=flops, bytes_accessed=moved, transcendentals=0),
            name=name,
        )(*args)
        self.last = results[-1]
        return results


def load_body(*refs):
    count = len(refs) // 2
    sems = refs[-1]
    copies = [pltpu.make_async_copy(refs[k], refs[count + k], sems.at[k]) for k in range(count)]
    for copy in copies:
        copy.start()
    for copy in copies:
        copy.wait()


def load_send_body(turn_ref, basis_ref, a_ref, b_ref, held, send_ref, rows_ref, sem, sems):
    blocks = fetch(basis_ref, held, sems)
    pick(turn_ref[0], b_ref, a_ref, rows_ref, sem)
    total = None
    for rows, copy in blocks:
        copy.wait()
        value = dot(rows_ref[:, rows], held[rows, :])
        total = value if total is None else total + value
    send_ref[...] = total.astype(NARROW)


def fetch(source, held, sems):
    count = sems.shape[0]
    size = source.shape[0] // count
    found = []
    for k in range(count):
        rows = pl.ds(k * size, size)
        copy = pltpu.make_async_copy(source.at[rows], held.at[rows], sems.at[k])
        copy.start()
        found.append((rows, copy))
    return found


def send_body(turn_ref, basis_ref, a_ref, b_ref, send_ref, rows_ref, sem):
    pick(turn_ref[0], b_ref, a_ref, rows_ref, sem)
    send_ref[...] = dot(rows_ref[...], basis_ref[...]).astype(NARROW)


def pick(turn, zero_ref, one_ref, rows_ref, sem):
    @pl.when(turn == 0)
    def _():
        copy = pltpu.make_async_copy(zero_ref, rows_ref, sem)
        copy.start()
        copy.wait()

    @pl.when(turn == 1)
    def _():
        copy = pltpu.make_async_copy(one_ref, rows_ref, sem)
        copy.start()
        copy.wait()


def pair_body(turn_ref, basis_ref, got_ref, a_ref, b_ref, out_ref, rows_ref, sem):
    pick(turn_ref[0], a_ref, b_ref, rows_ref, sem)
    out_ref[...] = (dot(rows_ref[...], basis_ref[...]) + got_ref[...].astype(WIDE)).astype(NARROW)


def pass_body(a_ref, out_ref):
    out_ref[...] = a_ref[...]


def mark_body(out_ref):
    out_ref[...] = jnp.zeros_like(out_ref)


def add_body(a_ref, b_ref, out_ref):
    out_ref[...] = (a_ref[...].astype(WIDE) + b_ref[...].astype(WIDE)).astype(NARROW)


def rotate_body(place_ref, b0, b1, b2, b3, basis_ref, mine_top, mine_low, top_ref, low_ref, rows_ref):
    size = b0.shape[0]
    half = 2 * size
    for k, block in enumerate((b0, b1, b2, b3)):
        rows_ref[pl.ds(pl.multiple_of(place_ref[k] * size, size), size), :] = block[...]
    core = place_ref[4]
    other = dot(rows_ref[pl.ds(pl.multiple_of((1 - core) * half, half), half), :], basis_ref[...])
    top_ref[...] = other[:size].astype(NARROW)
    low_ref[...] = other[size:].astype(NARROW)
    mine = dot(rows_ref[pl.ds(pl.multiple_of(core * half, half), half), :], basis_ref[...])
    mine_top[...] = mine[:size]
    mine_low[...] = mine[size:]


def chip_sum_body(core_ref, mine_ref, pair_ref, *refs):
    given = (len(refs) - 2) // 2
    wide_ref, out_ref = refs[given], refs[given + 1]
    size = out_ref.shape[0]
    source = pl.ds(pl.multiple_of((1 - core_ref[0]) * size, size), size)
    value = mine_ref[...] + pair_ref[source, :].astype(WIDE)
    wide_ref[...] = value
    out_ref[...] = value.astype(NARROW)
    for k in range(given):
        refs[given + 2 + k][...] = refs[k][...]


def panel_sum_body(wide_ref, got_ref, out_ref):
    out_ref[...] = (wide_ref[...] + got_ref[...].astype(WIDE)).astype(NARROW)


def score_body(
    spot_ref, a0, a1, a2, a3, mine_top, mine_low, other_top, other_low, query_ref, eig_ref, out_ref,
    act_ref, grad_ref, query_buf, eig_buf, sems
):
    depth, queries, cols = query_ref.shape
    owners = out_ref.shape[0]
    tokens = 4 * a0.shape[0]
    count = depth // LANES

    def copies(k):
        slot = lax.rem(k, SLOTS)
        rows = pl.ds(pl.multiple_of(k * LANES, LANES), LANES)
        return (
            pltpu.make_async_copy(query_ref.at[rows], query_buf.at[slot], sems.at[slot, 0]),
            pltpu.make_async_copy(eig_ref.at[rows], eig_buf.at[slot], sems.at[slot, 1]),
        )

    for k in range(SLOTS - 1):
        for copy in copies(k):
            copy.start()

    size = tokens // 4
    for k, block in enumerate((a0, a1, a2, a3)):
        act_ref[pl.ds(pl.multiple_of(spot_ref[k] * size, size), size), :] = block[...]
    core = spot_ref[4]
    for first, refs in ((core, (mine_top, mine_low)), (1 - core, (other_top, other_low))):
        for k, ref in enumerate(refs):
            grad_ref[pl.ds(pl.multiple_of((2 * first + k) * size, size), size), :] = ref[...]

    group = LANES // queries
    lane = lax.broadcasted_iota(jnp.int32, (tokens, LANES), 1) // queries

    def step(k, total):
        @pl.when(k + SLOTS - 1 < count)
        def _():
            for copy in copies(k + SLOTS - 1):
                copy.start()

        for copy in copies(k):
            copy.wait()
        slot = lax.rem(k, SLOTS)
        start = pl.multiple_of(k * LANES, LANES)
        scale = 1.0 / (eig_buf[slot] + DAMPING)
        query = query_buf[slot].astype(WIDE) * scale[:, None, :]
        precond = query.reshape(LANES * queries, cols).astype(NARROW)
        mixed = lax.dot_general(
            act_ref[...], precond, (((1,), (1,)), ((), ())), preferred_element_type=WIDE
        )
        grad = grad_ref[:, pl.ds(start, LANES)].astype(WIDE)
        for part in range(queries):
            spread = jnp.take_along_axis(grad, lane + part * group, axis=1)
            total = total + mixed[:, part * LANES : (part + 1) * LANES] * spread
        return total

    total = lax.fori_loop(0, count, step, jnp.zeros((tokens, LANES), WIDE))
    shift = LANES // 2
    while shift >= queries:
        total = total + pltpu.roll(total, shift, 1)
        shift //= 2
    turned = total.T[:queries, :]
    owned = tokens // owners
    for k in range(owners):
        out_ref[k, :, :owned] = turned[:, k * owned : (k + 1) * owned]


def final_body(got_ref, out_ref):
    out_ref[...] = jnp.sum(got_ref[...], axis=0)[:, : out_ref.shape[1]]


def spread_out(partial):
    queries, tokens = partial.shape
    owners = lax.axis_size("panel") * lax.axis_size("tok")
    split = partial.reshape(queries, owners, tokens // owners).transpose(1, 0, 2)
    return lax.all_to_all(split, ("panel", "tok"), split_axis=0, concat_axis=0, tiled=True)


def on_lines_of_four(grads, acts, out_basis, in_basis, query_rot, eigvals):
    size, feats = grads.shape
    depth, queries, cols = query_rot.shape
    panel, tok = lax.axis_index("panel"), lax.axis_index("tok")
    core, turn = panel % 2, (tok ^ tok // 2) % 2
    steps = Steps()

    def wide(*shape):
        return jax.ShapeDtypeStruct(shape, WIDE)

    def narrow(*shape):
        return jax.ShapeDtypeStruct(shape, NARROW)

    def scalars(*values):
        return jnp.stack(values).astype(jnp.int32)

    g1, g3 = swap(grads, "tok", 1), swap(grads, "tok", 2)
    near = swap(acts, "panel", 1)
    far = swap(acts, "panel", 2)
    most = swap(acts, "panel", 3)

    def loaded(name, *arrays):
        return steps(
            name, load_body, [], [narrow(*x.shape) for x in arrays],
            scratch=[pltpu.SemaphoreType.DMA((len(arrays),))], streamed=arrays,
        )

    one = [pltpu.VMEM((size, feats), NARROW), pltpu.SemaphoreType.DMA]
    cost = 2 * size * feats * cols
    options = dict(scalars=scalars(turn), scratch=one, flops=cost)
    acts = pltpu.with_memory_space_constraint(acts, pltpu.HBM)
    in_basis, send1 = steps(
        "send_near", load_send_body, [], [narrow(*in_basis.shape), narrow(size, cols)], scalars=scalars(turn),
        scratch=one + [pltpu.SemaphoreType.DMA((4,))], flops=cost, streamed=[in_basis], where=[acts, pltpu.with_memory_space_constraint(near, pltpu.HBM)],
    )
    got1 = swap(send1, "tok", 1)
    (g3,) = steps("pass", pass_body, [g3], [narrow(size, feats)], after=[g1])
    g2 = swap(g3, "tok", 1)
    (send2,) = steps("send_far", send_body, [in_basis], [narrow(size, cols)], where=[far, most], **options)
    got2 = swap(send2, "tok", 1)
    (pair1,) = steps("pair_near", pair_body, [in_basis, got1], [narrow(size, cols)], where=[acts, pltpu.with_memory_space_constraint(near, pltpu.HBM)], **options)
    got1 = swap(pair1, "tok", 3)
    (out_basis,) = loaded("load_out", out_basis)
    mine_top, mine_low, top, low = steps(
        "rotate", rotate_body, [grads, g1, g3, g2, out_basis], [wide(size, depth)] * 2 + [narrow(size, depth)] * 2,
        scalars=scalars(tok, tok ^ 1, tok ^ 2, tok ^ 3, core),
        scratch=[pltpu.VMEM((4 * size, feats), NARROW)], flops=8 * size * feats * depth,
    )
    chips = [[2 * k, 2 * k + 1] for k in range(2)]

    def chip_sum(name, mine, other, *handed):
        both = lax.all_gather(other, "panel", axis=0, tiled=True, axis_index_groups=chips)
        mine, other, *handed = steps(
            name, chip_sum_body, [mine, both, *handed],
            [wide(size, depth), narrow(size, depth)] + [narrow(size, depth)] * len(handed), scalars=scalars(core),
        )
        return mine, swap(other, "panel", 2), *handed

    mine_top, top, low = chip_sum("chip_sum_top", mine_top, top, low)
    (pair2,) = steps("pair_far", pair_body, [in_basis, got2], [narrow(size, cols)], where=[far, most], **options)
    got2 = swap(pair2, "tok", 3)
    (total1,) = steps("total_near", add_body, [pair1, got1], [narrow(size, cols)])
    back1 = swap(total1, "tok", 1)
    mine_low, low = chip_sum("chip_sum_low", mine_low, low)
    (total2,) = steps("total_far", add_body, [pair2, got2], [narrow(size, cols)])
    back2 = swap(total2, "tok", 1)
    (mine_top,) = steps("panel_sum_top", panel_sum_body, [mine_top, top], [narrow(size, depth)], after=[back1])
    other_top = swap(mine_top, "panel", 1)
    (mine_low,) = steps("panel_sum_low", panel_sum_body, [mine_low, low], [narrow(size, depth)])
    other_low = swap(mine_low, "panel", 1)
    steps("mark_far", mark_body, [], [wide(8, LANES)], after=[back2])
    owners = lax.axis_size("panel") * lax.axis_size("tok")
    (partial,) = steps(
        "scores", score_body, [total1, back1, total2, back2, mine_top, mine_low, other_top, other_low],
        [wide(owners, queries, LANES)],
        scalars=scalars(panel ^ turn, panel ^ turn ^ 1, panel ^ turn ^ 2, panel ^ turn ^ 3, core),
        scratch=[
            pltpu.VMEM((4 * size, cols), NARROW),
            pltpu.VMEM((4 * size, depth), NARROW),
            pltpu.VMEM((SLOTS, LANES, queries, cols), NARROW),
            pltpu.VMEM((SLOTS, LANES, cols), WIDE),
            pltpu.SemaphoreType.DMA((SLOTS, 2)),
        ],
        room=28 * 1024 * 1024, flops=8 * size * depth * queries * cols, streamed=[query_rot, eigvals],
    )
    got = lax.all_to_all(partial, ("panel", "tok"), split_axis=0, concat_axis=0, tiled=True)
    (out,) = steps("final", final_body, [got], [wide(queries, 4 * size // owners)])
    return out.T


def any_score_kernel(query_ref, eig_ref, act_ref, grad_ref, out_ref, act_turned, grad_turned):
    step = pl.program_id(0)
    block, queries, cols = query_ref.shape
    tokens = out_ref.shape[1]
    piece = math.gcd(block, 32)

    @pl.when(step == 0)
    def _():
        act_turned[...] = act_ref[...].astype(WIDE).T.astype(NARROW)
        grad_turned[...] = grad_ref[...].astype(WIDE).T
        out_ref[...] = jnp.zeros_like(out_ref)

    total = out_ref[...]
    for k in range(block // piece):
        scale = 1.0 / (eig_ref[k * piece : (k + 1) * piece, :] + DAMPING)
        query = query_ref[k * piece : (k + 1) * piece].astype(WIDE) * scale[:, None, :]
        precond = query.reshape(piece * queries, cols).astype(NARROW)
        mixed = dot(precond, act_turned[...]).reshape(piece, queries, tokens)
        grad = grad_turned[pl.ds(pl.multiple_of(step * block + k * piece, piece), piece), :]
        total = total + jnp.sum(mixed * grad[:, None, :], axis=0)
    out_ref[...] = total


def on_any(grads, acts, out_basis, in_basis, query_rot, eigvals):
    acts_all = lax.all_gather(acts, "panel", axis=0, tiled=True)
    grads_all = lax.all_gather(grads, "tok", axis=0, tiled=True)
    act_rot = lax.psum(dot(acts_all, in_basis), "tok").astype(NARROW)
    grad_rot = lax.psum(dot(grads_all, out_basis), "panel").astype(NARROW)
    depth, queries, cols = query_rot.shape
    tokens = act_rot.shape[0]
    step = math.gcd(depth, 256)
    partial = pl.pallas_call(
        any_score_kernel,
        grid=(depth // step,),
        in_specs=[
            pl.BlockSpec((step, queries, cols), lambda i: (i, 0, 0)),
            pl.BlockSpec((step, cols), lambda i: (i, 0)),
            IN_VMEM,
            IN_VMEM,
        ],
        out_specs=pl.BlockSpec((queries, tokens), lambda i: (0, 0)),
        out_shape=jax.ShapeDtypeStruct((queries, tokens), WIDE),
        scratch_shapes=[pltpu.VMEM((cols, tokens), NARROW), pltpu.VMEM((depth, tokens), WIDE)],
        compiler_params=pltpu.CompilerParams(vmem_limit_bytes=ROOM),
        name="any_scores",
    )(query_rot, eigvals, act_rot, grad_rot)
    return jnp.sum(spread_out(partial), axis=0).T


def per_device(*arrays):
    four = lax.axis_size("panel") == 4 and lax.axis_size("tok") == 4
    return (on_lines_of_four if four else on_any)(*arrays)


def solution(mesh):
    placed = (
        P(("groups", "tok"), "panel"),
        P(("groups", "panel"), "tok"),
        P("panel", "tok"),
        P("tok", "panel"),
        P("tok", None, "panel"),
        P("tok", "panel"),
    )
    return jax.shard_map(
        per_device,
        mesh=mesh,
        in_specs=placed,
        out_specs=P(("groups", "panel", "tok"), None),
        check_vma=False,
    )
```
